32 devices in a mesh: grp: 2 (over core), trk: 16 (over z, y, x).
Axes of the slice: x: 2, y: 2, z: 4, core: 2. Of those that a mesh axis runs over, the one named last changes fastest.
Arguments:
- fields: bfloat16 [32, 128, 512], P('grp', 'trk'), may hold values from -81 to 81
- upstream: bfloat16 [32, 128, 512], P('grp', 'trk'), may hold values from -6 to 6
- ln_gain: float32 [512], replicated, may hold values from 0.1 to 1.9
- weights: bfloat16 [4, 512, 512], P(None, 'grp', 'trk'), may hold values from -8 to 8
Outputs:
- grad_fields: bfloat16 [32, 128, 512], P('grp', 'trk')
- grad_weights: float32 [4, 512, 512], P(None, 'grp', 'trk')
- grad_gain: float32 [512], replicated
The draws below stay inside these ranges and needn't reach their ends.
All inputs are finite; a program needn't handle non-finite values.
Results may differ from the reference program's by a relative error of at most 0.014.
The reference program's roundings to bfloat16 on the way count: a program that leaves them out, or rounds other values in their place, can miss the bound.
Values may be sent and summed in bfloat16 or wider, within the bound.
No kernel may reach another device: no remote copies, remote signals or barrier semaphores. Data moves between devices by JAX's collectives and lax.ppermute only.
A program may use at most 64 MiB of HBM per device.

```python
import jax
import jax.numpy as jnp
from jax import lax

D = 512
HEADS = 8
TRACK = 128
HT = 32


def draw_fields(key, part):
    first_key = jax.random.fold_in(key, 0)
    values = jnp.clip(jax.random.normal(first_key, (HT, TRACK, D), jnp.float32), -8.0, 8.0)
    return values.astype(jnp.bfloat16)


def draw_weights(key, part):
    first_key = jax.random.fold_in(key, 0)
    values = jnp.clip(jax.random.normal(first_key, (4, D, D), jnp.float32), -6.0, 6.0) * D ** (-0.5)
    return values.astype(jnp.bfloat16)


def block_levels(stream_key, extent, cuts, least, largest):
    level = 1.0
    for axis_at, parts in cuts:
        steps = jax.random.uniform(jax.random.fold_in(jax.random.fold_in(stream_key, 6), axis_at), (parts,), jnp.float32, least / len(cuts), largest / len(cuts))
        level = level * jnp.repeat(jnp.exp(steps), extent[axis_at] // parts).reshape((-1,) + (1,) * (len(extent) - 1 - axis_at))
    return level


def scatter_about(stream_key, shape, scale, most, cuts=(), held_as=jnp.bfloat16):
    entries = jax.random.normal(stream_key, shape, jnp.float32) * scale
    if len(cuts) > 0:
        entries = block_levels(stream_key, shape, cuts, -0.22, 0.18) * entries
    return jnp.clip(entries, min=-most, max=most).astype(held_as)


def setup_inputs(seed: int = 0) -> dict:
    streams_of = jax.random.split(jax.random.key(seed), 5)
    return {
        "fields": draw_fields(jax.random.fold_in(streams_of[4], 71), 0),
        "upstream": scatter_about(streams_of[1], (HT, TRACK, D), 1.0, 6.0, ((0, 2), (1, 16))),
        "ln_gain": jnp.clip(1.0 + 0.18 * jax.random.normal(streams_of[2], (D,), jnp.float32), 0.1, 1.9),
        "weights": draw_weights(jax.random.fold_in(streams_of[4], 71), 0),
    }


def rounded(block):
    return lax.optimization_barrier(block.astype(jnp.bfloat16)).astype(jnp.float32)

def normalize(fields, ln_gain):
    values = fields.astype(jnp.float32)
    row_mean = lax.optimization_barrier(jnp.mean(values, -1, keepdims=True))
    offset = values - row_mean
    row_var = lax.optimization_barrier(jnp.mean(offset * offset, -1, keepdims=True))
    inv_std = lax.rsqrt(row_var + 1e-05)
    centred = offset * inv_std
    normed = (centred * ln_gain).astype(jnp.bfloat16)
    return (normed, centred, inv_std)

def split_heads(block):
    rows, length, width = block.shape
    return block.reshape(rows, length, HEADS, width // HEADS).transpose(0, 2, 1, 3).reshape(rows * HEADS, length, width // HEADS)

def merge_heads(block, rows):
    items, length, size = block.shape
    return block.reshape(rows, items // rows, length, size).transpose(0, 2, 1, 3).reshape(rows, length, items // rows * size)

def head_back(members):
    query, keyed, valued, grad_out = [member.astype(jnp.float32) for member in members]
    scaling = query.shape[-1] ** (-0.5)
    scores = jnp.einsum('qd,kd->qk', query, keyed) * scaling
    row_max = lax.optimization_barrier(jnp.max(scores, -1, keepdims=True))
    shifted = jnp.exp(scores - row_max)
    attn_prob = shifted / lax.optimization_barrier(jnp.sum(shifted, -1, keepdims=True))
    prob_low = rounded(attn_prob)
    output = jnp.einsum('qk,kd->qd', prob_low, valued).astype(jnp.bfloat16)
    dprobs = jnp.einsum('qd,kd->qk', grad_out, valued)
    row_dot = lax.optimization_barrier(jnp.sum(attn_prob * dprobs, -1, keepdims=True))
    score_grad = rounded(attn_prob * (dprobs - row_dot) * scaling)
    grad_value = jnp.einsum('qk,qd->kd', prob_low, grad_out).astype(jnp.bfloat16)
    grad_query = jnp.einsum('qk,kd->qd', score_grad, keyed).astype(jnp.bfloat16)
    grad_key = jnp.einsum('qk,qd->kd', score_grad, query).astype(jnp.bfloat16)
    return (output, grad_query, grad_key, grad_value)

def reference(fields, upstream, ln_gain, weights):
    rows, length, width = fields.shape
    normed, centred, inv_std = normalize(fields, ln_gain)
    flat = normed.reshape(-1, width)
    projected = [jnp.dot(flat, weights[index], preferred_element_type=jnp.float32).astype(jnp.bfloat16).reshape(rows, length, width) for index in range(3)]
    up_flat = upstream.reshape(-1, width)
    grad_attended = jnp.dot(up_flat, weights[3].T, preferred_element_type=jnp.float32).astype(jnp.bfloat16).reshape(rows, length, width)
    pieces = lax.map(head_back, (split_heads(projected[0]), split_heads(projected[1]), split_heads(projected[2]), split_heads(grad_attended)))
    attended, grad_query, grad_key, grad_value = [merge_heads(piece, rows).reshape(-1, width) for piece in pieces]
    raw_grad = jnp.stack([jnp.dot(flat.T, grad_query, preferred_element_type=jnp.float32), jnp.dot(flat.T, grad_key, preferred_element_type=jnp.float32), jnp.dot(flat.T, grad_value, preferred_element_type=jnp.float32), jnp.dot(attended.T, up_flat, preferred_element_type=jnp.float32)])
    stacked = jnp.stack([grad_query, grad_key, grad_value], 1).astype(jnp.float32)
    grad_normed = jnp.einsum('tcj,cij->ti', stacked, weights[:3].astype(jnp.float32)).reshape(rows, length, width)
    raw_gain = lax.optimization_barrier(jnp.sum((grad_normed * centred).reshape(-1, width), 0))
    scaled = grad_normed * ln_gain
    branch = inv_std * (scaled - lax.optimization_barrier(jnp.mean(scaled, -1, keepdims=True)) - centred * lax.optimization_barrier(jnp.mean(scaled * centred, -1, keepdims=True)))
    branch = branch.astype(jnp.bfloat16)
    grad_fields = (upstream.astype(jnp.float32) + branch.astype(jnp.float32)).astype(jnp.bfloat16)
    factor = float(rows * length) ** (-0.5)
    return (grad_fields, raw_grad * factor, raw_gain * factor)
```

```python
import functools

import jax
import jax.numpy as jnp
from jax import lax
from jax.experimental import pallas as pl
from jax.experimental.pallas import tpu as pltpu
from jax.sharding import PartitionSpec as P

HEADS = 8
BF = jnp.bfloat16
F32 = jnp.float32


def dot(a, b, dims):
    return lax.dot_general(a, b, (dims, ((), ())), preferred_element_type=F32)


def row_kernel(groups, place, rows_ref, gain_ref, *refs):
    w_refs, rest = refs[:groups], refs[groups:]
    wg_ref, cells_ref, w_all, norm_s, att_s = rest
    group, half_at = place[0], place[1]
    senders, pair, _ = rows_ref.shape
    tracks = pair // 2
    width = gain_ref.shape[1]
    length = senders * tracks
    fan, halves, _, cols, part = w_refs[0].shape
    both = rows_ref[...].astype(F32)
    values = both[:, :tracks].reshape(length, width)
    upstream = both[:, tracks:].reshape(length, width)
    gain = gain_ref[...]
    for step in range(groups):
        owner = lax.rem(group - step + groups, groups)
        lanes = pl.ds(pl.multiple_of(owner * part, part), part)
        for far in range(halves):
            base = lax.rem(half_at + far, halves) * (fan * cols)
            for near in range(fan):
                at = pl.ds(pl.multiple_of(base + near * cols, cols), cols)
                for index in range(4):
                    w_all[index, at, lanes] = w_refs[step][near, far, index]
    row_mean = jnp.mean(values, -1, keepdims=True)
    offset = values - row_mean
    row_var = jnp.mean(offset * offset, -1, keepdims=True)
    inv_std = lax.rsqrt(row_var + 1e-05)
    centred = offset * inv_std
    normed = (centred * gain).astype(BF)
    up = upstream.astype(BF)
    projected = [dot(normed, w_all[index], ((1,), (1,))).astype(BF) for index in range(3)]
    grad_att = dot(up, w_all[3], ((1,), (0,))).astype(BF)
    size = width // HEADS
    scaling = size ** (-0.5)
    span = 2 * size
    lane = lax.broadcasted_iota(jnp.int32, (length, span), 1)
    first = lane < size
    pieces = [[], [], [], []]
    for at in range(0, width, span):
        query, keyed, valued = [member[:, at : at + span] for member in projected]
        grad_out = grad_att[:, at : at + span]
        zero = jnp.zeros_like(query)
        query2 = jnp.concatenate([jnp.where(first, query, zero), jnp.where(first, zero, query)], 0)
        grad2 = jnp.concatenate(
            [jnp.where(first, grad_out, zero), jnp.where(first, zero, grad_out)], 0
        )
        scores = dot(query2, keyed, ((1,), (1,))) * scaling
        shifted = jnp.exp(scores - jnp.max(scores, -1, keepdims=True))
        prob = shifted / jnp.sum(shifted, -1, keepdims=True)
        prob_low = prob.astype(BF)
        dprobs = dot(grad2, valued, ((1,), (1,)))
        row_dot = jnp.sum(prob * dprobs, -1, keepdims=True)
        score_grad = (prob * (dprobs - row_dot) * scaling).astype(BF)
        out2 = dot(prob_low, valued, ((1,), (0,)))
        gq2 = dot(score_grad, keyed, ((1,), (0,)))
        pieces[0].append(jnp.where(first, gq2[:length], gq2[length:]).astype(BF))
        pieces[1].append(dot(score_grad, query2, ((0,), (0,))).astype(BF))
        pieces[2].append(dot(prob_low, grad2, ((0,), (0,))).astype(BF))
        pieces[3].append(jnp.where(first, out2[:length], out2[length:]).astype(BF))
    grads = [jnp.concatenate(piece, 1) for piece in pieces[:3]]
    attended = jnp.concatenate(pieces[3], 1)
    grad_normed = sum(dot(grads[index], w_all[index], ((1,), (0,))) for index in range(3))
    gain_term = jnp.sum(grad_normed * centred, 0, keepdims=True)
    scaled = grad_normed * gain
    branch = inv_std * (
        scaled
        - jnp.mean(scaled, -1, keepdims=True)
        - centred * jnp.mean(scaled * centred, -1, keepdims=True)
    )
    cells = upstream + branch.astype(BF).astype(F32)
    high = gain_term.astype(BF).astype(F32)
    low = gain_term - high
    which = lax.broadcasted_iota(jnp.int32, (tracks, width), 0)
    extra = jnp.where(which == 0, high, jnp.where(which == 1, low, 0.0))
    extra = jnp.broadcast_to(extra[None], (senders, tracks, width))
    cells_ref[...] = jnp.concatenate(
        [cells.reshape(senders, tracks, width), extra], 1
    ).astype(BF)
    for at in range(groups):
        norm_s[at] = normed[:, at * part : (at + 1) * part]
        att_s[at] = attended[:, at * part : (at + 1) * part]
    for step in range(groups):
        owner = lax.rem(group + step, groups)
        norm_part, att_part = norm_s[owner], att_s[owner]
        for index in range(4):
            if index < 3:
                block = dot(grads[index], norm_part, ((0,), (0,))).astype(BF)
            else:
                block = dot(up, att_part, ((0,), (0,))).astype(BF)
            block = block.reshape(halves, fan, cols, part)
            for far in range(halves):
                to = lax.rem(half_at + far, halves)
                for near in range(fan):
                    wg_ref[step, near, to, index] = block[far, near]


def ring(size, step):
    return [(i, (i + step) % size) for i in range(size)]


def join_blocks(blocks, half_at):
    fan, halves, four, cols, part = blocks.shape
    blocks = jnp.where(half_at == 0, blocks, blocks[:, ::-1])
    return blocks.transpose(2, 1, 0, 3, 4).reshape(1, 1, four, halves * fan * cols, part)


def cut_blocks(joined, half_at, shape):
    fan, halves, four, cols, part = shape
    blocks = joined.reshape(-1, four, halves, fan, cols, part).transpose(0, 3, 2, 1, 4, 5)
    return jnp.where(half_at == 0, blocks, blocks[:, :, ::-1])


def shards(fields, upstream, ln_gain, weights):
    groups, count = lax.axis_size("grp"), lax.axis_size("trk")
    rows_dev, trk_dev, width = fields.shape
    _, part, cols = weights.shape
    cell_count = rows_dev * groups * trk_dev * count
    fan = count // 2
    near = [[half * fan + i for i in range(fan)] for half in range(2)]
    group, track = lax.axis_index("grp"), lax.axis_index("trk")
    half_at = track // fan
    both = jnp.concatenate([fields, upstream], 1)
    row = lax.all_to_all(both, "trk", split_axis=0, concat_axis=0, tiled=True)
    own = weights.transpose(0, 2, 1)
    held = jnp.stack([own, lax.ppermute(own, "trk", ring(count, fan))])
    sent = jnp.broadcast_to(held[None], (fan,) + held.shape)
    w_part = lax.all_to_all(
        sent, "trk", split_axis=0, concat_axis=0, tiled=True, axis_index_groups=near
    )
    w_parts = [w_part] + [lax.ppermute(w_part, "grp", ring(groups, k)) for k in range(1, groups)]
    blocks_shape = w_part.shape
    narrow = cols % 16 != 0
    if narrow:
        w_parts = [join_blocks(blocks, half_at) for blocks in w_parts]
    place = jnp.stack([group, half_at]).astype(jnp.int32)
    vmem = pl.BlockSpec(memory_space=pltpu.VMEM)
    wg, cells = pl.pallas_call(
        functools.partial(row_kernel, groups),
        out_shape=(
            jax.ShapeDtypeStruct((groups,) + w_parts[0].shape, BF),
            jax.ShapeDtypeStruct((count, 2 * trk_dev, width), BF),
        ),
        in_specs=[pl.BlockSpec(memory_space=pltpu.SMEM)] + [vmem] * (2 + groups),
        out_specs=(vmem, vmem),
        scratch_shapes=[
            pltpu.VMEM((4, width, width), BF),
            pltpu.VMEM((groups, trk_dev * count, part), BF),
            pltpu.VMEM((groups, trk_dev * count, part), BF),
        ],
        compiler_params=pltpu.CompilerParams(vmem_limit_bytes=48 * 2**20),
    )(place, row, ln_gain[None], *w_parts)
    if narrow:
        wg = cut_blocks(wg, half_at, blocks_shape)
    total = wg[0].astype(F32)
    for k in range(1, groups):
        total = total + lax.ppermute(wg[k], "grp", ring(groups, k)).astype(F32)
    back = lax.all_to_all(cells, "trk", split_axis=0, concat_axis=0, tiled=True)
    spread = lax.all_to_all(
        total.astype(BF), "trk", split_axis=0, concat_axis=0, tiled=True, axis_index_groups=near
    )
    summed = jnp.sum(spread.astype(F32), 0)
    total = summed[0] + lax.ppermute(summed[1].astype(BF), "trk", ring(count, fan)).astype(F32)
    grad_fields = back[:, :trk_dev]
    gain_sum = jnp.sum(back[:, trk_dev : trk_dev + 2].astype(F32), (0, 1))
    gain_sum = lax.psum(gain_sum, "grp")
    factor = float(cell_count) ** (-0.5)
    return (grad_fields, total.transpose(0, 2, 1) * factor, gain_sum * factor)


def solution(mesh):
    in_specs = (P("grp", "trk", None), P("grp", "trk", None), P(), P(None, "grp", "trk"))
    out_specs = (P("grp", "trk", None), P(None, "grp", "trk"), P())
    return jax.shard_map(shards, mesh=mesh, in_specs=in_specs, out_specs=out_specs, check_vma=False)
```

```python
import functools

import jax
import jax.numpy as jnp
from jax import lax
from jax.experimental import pallas as pl
from jax.experimental.pallas import tpu as pltpu
from jax.sharding import PartitionSpec as P

HEADS = 8
BF = jnp.bfloat16
F32 = jnp.float32


def dot(a, b, dims):
    return lax.dot_general(a, b, (dims, ((), ())), preferred_element_type=F32)


def row_kernel(groups, offsets, place, rows_ref, gain_ref, *refs):
    w_refs, rest = refs[: groups * len(offsets)], refs[groups * len(offsets) :]
    wg_refs, cells_ref, (w_all, norm_s, att_s, sems) = rest[:groups], rest[groups], rest[groups + 1 :]
    group, track = place[0], place[1]
    senders, pair, _ = rows_ref.shape
    tracks = pair // 2
    width = gain_ref.shape[1]
    length = senders * tracks
    fan, halves, _, cols, part = wg_refs[0].shape
    half_at = track // fan
    copies = []
    for step in range(groups):
        owner = lax.rem(group - step + groups, groups)
        lanes = pl.ds(pl.multiple_of(owner * part, part), part)
        for at, held in enumerate(offsets):
            for slot, offset in enumerate(held):
                size = w_refs[0].shape[2]
                begin = (track ^ offset) * size if len(offsets) > 1 else 0
                rows = pl.ds(pl.multiple_of(begin, size), size)
                copy = pltpu.make_async_copy(
                    w_refs[step * len(offsets) + at].at[slot],
                    w_all.at[:, rows, lanes],
                    sems.at[len(copies)],
                )
                copy.start()
                copies.append(copy)
    both = rows_ref[...].astype(F32)
    values = both[:, :tracks].reshape(length, width)
    upstream = both[:, tracks:].reshape(length, width)
    gain = gain_ref[...]
    row_mean = jnp.mean(values, -1, keepdims=True)
    offset = values - row_mean
    row_var = jnp.mean(offset * offset, -1, keepdims=True)
    inv_std = lax.rsqrt(row_var + 1e-05)
    centred = offset * inv_std
    normed = (centred * gain).astype(BF)
    up = upstream.astype(BF)
    for copy in copies:
        copy.wait()
    projected = [dot(normed, w_all[index], ((1,), (1,))).astype(BF) for index in range(3)]
    grad_att = dot(up, w_all[3], ((1,), (0,))).astype(BF)
    size = width // HEADS
    scaling = size ** (-0.5)
    span = 2 * size
    lane = lax.broadcasted_iota(jnp.int32, (length, span), 1)
    first = lane < size
    pieces = [[], [], [], []]
    for at in range(0, width, span):
        query, keyed, valued = [member[:, at : at + span] for member in projected]
        grad_out = grad_att[:, at : at + span]
        zero = jnp.zeros_like(query)
        query2 = jnp.concatenate([jnp.where(first, query, zero), jnp.where(first, zero, query)], 0)
        grad2 = jnp.concatenate(
            [jnp.where(first, grad_out, zero), jnp.where(first, zero, grad_out)], 0
        )
        scores = dot(query2, keyed, ((1,), (1,))) * scaling
        shifted = jnp.exp(scores - jnp.max(scores, -1, keepdims=True))
        prob = shifted / jnp.sum(shifted, -1, keepdims=True)
        prob_low = prob.astype(BF)
        dprobs = dot(grad2, valued, ((1,), (1,)))
        row_dot = jnp.sum(prob * dprobs, -1, keepdims=True)
        score_grad = (prob * (dprobs - row_dot) * scaling).astype(BF)
        out2 = dot(prob_low, valued, ((1,), (0,)))
        gq2 = dot(score_grad, keyed, ((1,), (0,)))
        pieces[0].append(jnp.where(first, gq2[:length], gq2[length:]).astype(BF))
        pieces[1].append(dot(score_grad, query2, ((0,), (0,))).astype(BF))
        pieces[2].append(dot(prob_low, grad2, ((0,), (0,))).astype(BF))
        pieces[3].append(jnp.where(first, out2[:length], out2[length:]).astype(BF))
    grads = [jnp.concatenate(piece, 1) for piece in pieces[:3]]
    attended = jnp.concatenate(pieces[3], 1)
    grad_normed = sum(dot(grads[index], w_all[index], ((1,), (0,))) for index in range(3))
    gain_term = jnp.sum(grad_normed * centred, 0, keepdims=True)
    scaled = grad_normed * gain
    branch = inv_std * (
        scaled
        - jnp.mean(scaled, -1, keepdims=True)
        - centred * jnp.mean(scaled * centred, -1, keepdims=True)
    )
    cells = upstream + branch.astype(BF).astype(F32)
    high = gain_term.astype(BF).astype(F32)
    low = gain_term - high
    which = lax.broadcasted_iota(jnp.int32, (tracks, width), 0)
    extra = jnp.where(which == 0, high, jnp.where(which == 1, low, 0.0))
    extra = jnp.broadcast_to(extra[None], (senders, tracks, width))
    cells_ref[...] = jnp.concatenate(
        [cells.reshape(senders, tracks, width), extra], 1
    ).astype(BF)
    for at in range(groups):
        norm_s[at] = normed[:, at * part : (at + 1) * part]
        att_s[at] = attended[:, at * part : (at + 1) * part]
    for step in range(groups):
        owner = lax.rem(group + step, groups)
        norm_part, att_part = norm_s[owner], att_s[owner]
        for index in range(4):
            if index < 3:
                block = dot(grads[index], norm_part, ((0,), (0,))).astype(BF)
            else:
                block = dot(up, att_part, ((0,), (0,))).astype(BF)
            block = block.reshape(halves, fan, cols, part)
            for far in range(halves):
                to = lax.rem(half_at + far, halves)
                for near in range(fan):
                    wg_refs[step][near, to, index] = block[far, near]


def ring(size, step):
    return [(i, (i + step) % size) for i in range(size)]


def join_blocks(parts, offsets, track):
    blocks = jnp.concatenate(parts)
    order = [offset for held in offsets for offset in held]
    where = [order.index(offset) for offset in range(len(order))]
    blocks = jnp.take(blocks, jnp.array(where)[track ^ jnp.arange(len(order))], axis=0)
    count, four, cols, part = blocks.shape
    return blocks.transpose(1, 0, 2, 3).reshape(1, four, count * cols, part)


def cut_blocks(joined, half_at, shape):
    fan, halves, four, cols, part = shape
    blocks = joined.reshape(four, halves, fan, cols, part).transpose(2, 1, 0, 3, 4)
    return jnp.where(half_at == 0, blocks, blocks[:, ::-1])


def gather_blocks(block, axis):
    count = lax.axis_size(axis)

    def swap(array, bits):
        return lax.ppermute(array, axis, [(i, i ^ bits) for i in range(count)])

    held, order, bit = block[None], [0], count // 2
    while bit >= 4:
        held = jnp.concatenate([held, swap(held, bit)])
        order = order + [offset ^ bit for offset in order]
        bit //= 2
    close = range(2 * bit)
    parts = [swap(held, bits) if bits else held for bits in close]
    return parts, [[offset ^ bits for offset in order] for bits in close]


def shards(fields, upstream, ln_gain, weights):
    groups, count = lax.axis_size("grp"), lax.axis_size("trk")
    rows_dev, trk_dev, width = fields.shape
    _, part, cols = weights.shape
    cell_count = rows_dev * groups * trk_dev * count
    fan = count // 2
    near = [[half * fan + i for i in range(fan)] for half in range(2)]
    group, track = lax.axis_index("grp"), lax.axis_index("trk")
    half_at = track // fan
    both = jnp.concatenate([fields, upstream], 1)
    row = lax.all_to_all(both, "trk", split_axis=0, concat_axis=0, tiled=True)
    parts, offsets = gather_blocks(weights.transpose(0, 2, 1), "trk")
    blocks_shape = (fan, 2, 4, cols, part)
    out_shape = blocks_shape
    narrow = cols % 16 != 0
    if narrow:
        parts, offsets = [join_blocks(parts, offsets, track)], [[0]]
        out_shape = (1, 1, 4, count * cols, part)
    w_parts = [
        lax.ppermute(held, "grp", ring(groups, k)) if k else held
        for k in range(groups)
        for held in parts
    ]
    place = jnp.stack([group, track]).astype(jnp.int32)
    vmem = pl.BlockSpec(memory_space=pltpu.VMEM)
    *wg, cells = pl.pallas_call(
        functools.partial(row_kernel, groups, offsets),
        out_shape=(jax.ShapeDtypeStruct(out_shape, BF),) * groups
        + (jax.ShapeDtypeStruct((count, 2 * trk_dev, width), BF),),
        in_specs=[pl.BlockSpec(memory_space=pltpu.SMEM), vmem, vmem]
        + [pl.BlockSpec(memory_space=pl.ANY)] * len(w_parts),
        out_specs=(vmem,) * (groups + 1),
        scratch_shapes=[
            pltpu.VMEM((4, width, width), BF),
            pltpu.VMEM((groups, trk_dev * count, part), BF),
            pltpu.VMEM((groups, trk_dev * count, part), BF),
            pltpu.SemaphoreType.DMA((groups * sum(len(held) for held in offsets),)),
        ],
        compiler_params=pltpu.CompilerParams(vmem_limit_bytes=48 * 2**20),
    )(place, row, ln_gain[None], *w_parts)
    if narrow:
        wg = [cut_blocks(blocks, half_at, blocks_shape) for blocks in wg]
    total = wg[0].astype(F32)
    for k in range(1, groups):
        total = total + lax.ppermute(wg[k], "grp", ring(groups, k)).astype(F32)
    back = lax.all_to_all(cells, "trk", split_axis=0, concat_axis=0, tiled=True)
    spread = lax.all_to_all(
        total.astype(BF), "trk", split_axis=0, concat_axis=0, tiled=True, axis_index_groups=near
    )
    summed = jnp.sum(spread.astype(F32), 0)
    total = summed[0] + lax.ppermute(summed[1].astype(BF), "trk", ring(count, fan)).astype(F32)
    grad_fields = back[:, :trk_dev]
    gain_sum = jnp.sum(back[:, trk_dev : trk_dev + 2].astype(F32), (0, 1))
    gain_sum = lax.psum(gain_sum, "grp")
    factor = float(cell_count) ** (-0.5)
    return (grad_fields, total.transpose(0, 2, 1) * factor, gain_sum * factor)


def solution(mesh):
    in_specs = (P("grp", "trk", None), P("grp", "trk", None), P(), P(None, "grp", "trk"))
    out_specs = (P("grp", "trk", None), P(None, "grp", "trk"), P())
    return jax.shard_map(shards, mesh=mesh, in_specs=in_specs, out_specs=out_specs, check_vma=False)
```

```python
import functools

import jax
import jax.numpy as jnp
from jax import lax
from jax.experimental import pallas as pl
from jax.experimental.pallas import tpu as pltpu
from jax.sharding import PartitionSpec as P

HEADS = 8
BF = jnp.bfloat16
F32 = jnp.float32


def dot(a, b, dims):
    return lax.dot_general(a, b, (dims, ((), ())), preferred_element_type=F32)


def send_slot(offset, count):
    slot, bit = offset & 3, 4
    while bit < count:
        slot = slot * 2 + (offset // bit) % 2
        bit *= 2
    return slot


def row_kernel(groups, offsets, place, rows_ref, gain_ref, *refs):
    w_refs, rest = refs[: groups * len(offsets)], refs[groups * len(offsets) :]
    wg_refs, cells_ref, (w_all, norm_s, att_s, sems) = rest[:groups], rest[groups], rest[groups + 1 :]
    group, track = place[0], place[1]
    senders, pair, _ = rows_ref.shape
    tracks = pair // 2
    width = gain_ref.shape[1]
    length = senders * tracks
    count, _, cols, part = wg_refs[0].shape
    copies = []
    for step in range(groups):
        owner = lax.rem(group - step + groups, groups)
        lanes = pl.ds(pl.multiple_of(owner * part, part), part)
        for at, held in enumerate(offsets):
            for slot, offset in enumerate(held):
                size = w_refs[0].shape[2]
                begin = (track ^ offset) * size if len(offsets) > 1 else 0
                rows = pl.ds(pl.multiple_of(begin, size), size)
                copy = pltpu.make_async_copy(
                    w_refs[step * len(offsets) + at].at[slot],
                    w_all.at[:, rows, lanes],
                    sems.at[len(copies)],
                )
                copy.start()
                copies.append(copy)
    both = rows_ref[...].astype(F32)
    values = both[:, :tracks].reshape(length, width)
    upstream = both[:, tracks:].reshape(length, width)
    gain = gain_ref[...]
    row_mean = jnp.mean(values, -1, keepdims=True)
    offset = values - row_mean
    row_var = jnp.mean(offset * offset, -1, keepdims=True)
    inv_std = lax.rsqrt(row_var + 1e-05)
    centred = offset * inv_std
    normed = (centred * gain).astype(BF)
    up = upstream.astype(BF)
    for copy in copies:
        copy.wait()
    projected = [dot(normed, w_all[index], ((1,), (1,))).astype(BF) for index in range(3)]
    grad_att = dot(up, w_all[3], ((1,), (0,))).astype(BF)
    size = width // HEADS
    scaling = size ** (-0.5)
    span = 2 * size
    lane = lax.broadcasted_iota(jnp.int32, (length, span), 1)
    first = lane < size
    pieces = [[], [], [], []]
    for at in range(0, width, span):
        query, keyed, valued = [member[:, at : at + span] for member in projected]
        grad_out = grad_att[:, at : at + span]
        zero = jnp.zeros_like(query)
        query2 = jnp.concatenate([jnp.where(first, query, zero), jnp.where(first, zero, query)], 0)
        grad2 = jnp.concatenate(
            [jnp.where(first, grad_out, zero), jnp.where(first, zero, grad_out)], 0
        )
        scores = dot(query2, keyed, ((1,), (1,))) * scaling
        shifted = jnp.exp(scores - jnp.max(scores, -1, keepdims=True))
        prob = shifted / jnp.sum(shifted, -1, keepdims=True)
        prob_low = prob.astype(BF)
        dprobs = dot(grad2, valued, ((1,), (1,)))
        row_dot = jnp.sum(prob * dprobs, -1, keepdims=True)
        score_grad = (prob * (dprobs - row_dot) * scaling).astype(BF)
        out2 = dot(prob_low, valued, ((1,), (0,)))
        gq2 = dot(score_grad, keyed, ((1,), (0,)))
        pieces[0].append(jnp.where(first, gq2[:length], gq2[length:]).astype(BF))
        pieces[1].append(dot(score_grad, query2, ((0,), (0,))).astype(BF))
        pieces[2].append(dot(prob_low, grad2, ((0,), (0,))).astype(BF))
        pieces[3].append(jnp.where(first, out2[:length], out2[length:]).astype(BF))
    grads = [jnp.concatenate(piece, 1) for piece in pieces[:3]]
    attended = jnp.concatenate(pieces[3], 1)
    grad_normed = sum(dot(grads[index], w_all[index], ((1,), (0,))) for index in range(3))
    gain_term = jnp.sum(grad_normed * centred, 0, keepdims=True)
    scaled = grad_normed * gain
    branch = inv_std * (
        scaled
        - jnp.mean(scaled, -1, keepdims=True)
        - centred * jnp.mean(scaled * centred, -1, keepdims=True)
    )
    cells = upstream + branch.astype(BF).astype(F32)
    high = gain_term.astype(BF).astype(F32)
    low = gain_term - high
    which = lax.broadcasted_iota(jnp.int32, (tracks, width), 0)
    extra = jnp.where(which == 0, high, jnp.where(which == 1, low, 0.0))
    extra = jnp.broadcast_to(extra[None], (senders, tracks, width))
    cells_ref[...] = jnp.concatenate(
        [cells.reshape(senders, tracks, width), extra], 1
    ).astype(BF)
    for at in range(groups):
        norm_s[at] = normed[:, at * part : (at + 1) * part]
        att_s[at] = attended[:, at * part : (at + 1) * part]
    for step in range(groups):
        owner = lax.rem(group + step, groups)
        norm_part, att_part = norm_s[owner], att_s[owner]
        for index in range(4):
            if index < 3:
                block = dot(grads[index], norm_part, ((0,), (0,))).astype(BF)
            else:
                block = dot(up, att_part, ((0,), (0,))).astype(BF)
            block = block.reshape(count, cols, part)
            for to in range(count):
                slot = send_slot(track ^ to, count) if count > 1 else 0
                wg_refs[step][slot, index] = block[to]


def ring(size, step):
    return [(i, (i + step) % size) for i in range(size)]


def swap(array, axis, bits):
    return lax.ppermute(array, axis, [(i, i ^ bits) for i in range(lax.axis_size(axis))])


def join_blocks(parts, offsets, track):
    blocks = jnp.concatenate(parts)
    order = [offset for held in offsets for offset in held]
    where = [order.index(offset) for offset in range(len(order))]
    blocks = jnp.take(blocks, jnp.array(where)[track ^ jnp.arange(len(order))], axis=0)
    count, four, cols, part = blocks.shape
    return blocks.transpose(1, 0, 2, 3).reshape(1, four, count * cols, part)


def cut_blocks(joined, count, track):
    _, four, width, part = joined.shape
    blocks = joined.reshape(four, count, width // count, part).transpose(1, 0, 2, 3)
    slots = [send_slot(offset, count) for offset in range(count)]
    order = [slots.index(slot) for slot in range(count)]
    return jnp.take(blocks, track ^ jnp.array(order), axis=0)


def gather_blocks(block, axis, other):
    count = lax.axis_size(axis)
    held, order, bit = block[None], [0], count // 2
    while bit >= 4:
        moved = swap(held, axis, bit)
        if len(order) == 1:
            moved, other = lax.optimization_barrier((moved, other))
        held = jnp.concatenate([held, moved])
        order = order + [offset ^ bit for offset in order]
        bit //= 2
    close = range(2 * bit)
    parts = [swap(held, axis, bits) if bits else held for bits in close]
    return parts, [[offset ^ bits for offset in order] for bits in close], other


def scatter_sum(blocks, axis):
    count = lax.axis_size(axis)
    blocks = blocks.reshape((4, count // 4) + blocks.shape[1:])
    moved = [swap(blocks[bits], axis, bits) for bits in (1, 2, 3)]
    total = blocks[0].astype(F32) + sum(block.astype(F32) for block in moved)
    bit = 4
    while bit < count:
        half = total.shape[0] // 2
        total = total[:half] + swap(total[half:].astype(BF), axis, bit).astype(F32)
        bit *= 2
    return total[0]


def shards(fields, upstream, ln_gain, weights):
    groups, count = lax.axis_size("grp"), lax.axis_size("trk")
    rows_dev, trk_dev, width = fields.shape
    _, part, cols = weights.shape
    cell_count = rows_dev * groups * trk_dev * count
    group, track = lax.axis_index("grp"), lax.axis_index("trk")
    both = jnp.concatenate([fields, upstream], 1)
    parts, offsets, both = gather_blocks(weights.transpose(0, 2, 1), "trk", both)
    row = lax.all_to_all(both, "trk", split_axis=0, concat_axis=0, tiled=True)
    out_shape = (count, 4, cols, part)
    narrow = cols % 16 != 0
    if narrow:
        parts, offsets = [join_blocks(parts, offsets, track)], [[0]]
        out_shape = (1, 4, count * cols, part)
    w_parts = [
        lax.ppermute(held, "grp", ring(groups, k)) if k else held
        for k in range(groups)
        for held in parts
    ]
    place = jnp.stack([group, track]).astype(jnp.int32)
    vmem = pl.BlockSpec(memory_space=pltpu.VMEM)
    *wg, cells = pl.pallas_call(
        functools.partial(row_kernel, groups, offsets),
        out_shape=(jax.ShapeDtypeStruct(out_shape, BF),) * groups
        + (jax.ShapeDtypeStruct((count, 2 * trk_dev, width), BF),),
        in_specs=[pl.BlockSpec(memory_space=pltpu.SMEM), vmem, vmem]
        + [pl.BlockSpec(memory_space=pl.ANY)] * len(w_parts),
        out_specs=(vmem,) * (groups + 1),
        scratch_shapes=[
            pltpu.VMEM((4, width, width), BF),
            pltpu.VMEM((groups, trk_dev * count, part), BF),
            pltpu.VMEM((groups, trk_dev * count, part), BF),
            pltpu.SemaphoreType.DMA((groups * sum(len(held) for held in offsets),)),
        ],
        compiler_params=pltpu.CompilerParams(vmem_limit_bytes=48 * 2**20),
    )(place, row, ln_gain[None], *w_parts)
    if narrow:
        wg = [cut_blocks(blocks, count, track) for blocks in wg]
    back = lax.all_to_all(cells, "trk", split_axis=0, concat_axis=0, tiled=True)
    total = wg[0].astype(F32)
    for k in range(1, groups):
        total = total + lax.ppermute(wg[k], "grp", ring(groups, k)).astype(F32)
    total = scatter_sum(total.astype(BF), "trk")
    grad_fields = back[:, :trk_dev]
    gain_sum = jnp.sum(back[:, trk_dev : trk_dev + 2].astype(F32), (0, 1))
    if groups == 2:
        gain_sum = gain_sum + lax.ppermute(gain_sum, "grp", ring(2, 1))
    else:
        gain_sum = jnp.sum(lax.all_gather(gain_sum, "grp"), 0)
    factor = float(cell_count) ** (-0.5)
    return (grad_fields, total.transpose(0, 2, 1) * factor, gain_sum * factor)


def solution(mesh):
    in_specs = (P("grp", "trk", None), P("grp", "trk", None), P(), P(None, "grp", "trk"))
    out_specs = (P("grp", "trk", None), P(None, "grp", "trk"), P())
    return jax.shard_map(shards, mesh=mesh, in_specs=in_specs, out_specs=out_specs, check_vma=False)
```

```python
import functools

import jax
import jax.numpy as jnp
from jax import lax
from jax.experimental import pallas as pl
from jax.experimental.pallas import tpu as pltpu
from jax.sharding import PartitionSpec as P

HEADS = 8
BF = jnp.bfloat16
F32 = jnp.float32


def dot(a, b, dims):
    return lax.dot_general(a, b, (dims, ((), ())), preferred_element_type=F32)


def send_slot(offset, count):
    slot, bit = offset & 3, 4
    while bit < count:
        slot = slot * 2 + (offset // bit) % 2
        bit *= 2
    return slot


def row_kernel(groups, offsets, place, rows_ref, gain_ref, *refs):
    w_refs, rest = refs[: groups * len(offsets)], refs[groups * len(offsets) :]
    wg_refs, cells_ref, (w_all, norm_s, att_s, sems) = rest[:groups], rest[groups], rest[groups + 1 :]
    group, track = place[0], place[1]
    senders, pair, _ = rows_ref.shape
    tracks = pair // 2
    width = gain_ref.shape[1]
    length = senders * tracks
    count, _, cols, part = wg_refs[0].shape
    copies = []
    for step in range(groups):
        owner = lax.rem(group - step + groups, groups)
        lanes = pl.ds(pl.multiple_of(owner * part, part), part)
        for at, held in enumerate(offsets):
            for slot, offset in enumerate(held):
                size = w_refs[0].shape[2]
                begin = (track ^ offset) * size if len(offsets) > 1 else 0
                rows = pl.ds(pl.multiple_of(begin, size), size)
                copy = pltpu.make_async_copy(
                    w_refs[step * len(offsets) + at].at[slot],
                    w_all.at[:, rows, lanes],
                    sems.at[len(copies)],
                )
                copy.start()
                copies.append(copy)
    both = rows_ref[...].astype(F32)
    values = both[:, :tracks].reshape(length, width)
    upstream = both[:, tracks:].reshape(length, width)
    gain = gain_ref[...]
    row_mean = jnp.mean(values, -1, keepdims=True)
    offset = values - row_mean
    row_var = jnp.mean(offset * offset, -1, keepdims=True)
    inv_std = lax.rsqrt(row_var + 1e-05)
    centred = offset * inv_std
    normed = (centred * gain).astype(BF)
    up = upstream.astype(BF)
    for copy in copies:
        copy.wait()
    projected = [dot(normed, w_all[index], ((1,), (1,))).astype(BF) for index in range(3)]
    grad_att = dot(up, w_all[3], ((1,), (0,))).astype(BF)
    size = width // HEADS
    scaling = size ** (-0.5)
    span = 2 * size
    lane = lax.broadcasted_iota(jnp.int32, (length, span), 1)
    first = lane < size
    pieces = [[], [], [], []]
    for at in range(0, width, span):
        query, keyed, valued = [member[:, at : at + span] for member in projected]
        grad_out = grad_att[:, at : at + span]
        zero = jnp.zeros_like(query)
        query2 = jnp.concatenate([jnp.where(first, query, zero), jnp.where(first, zero, query)], 0)
        grad2 = jnp.concatenate(
            [jnp.where(first, grad_out, zero), jnp.where(first, zero, grad_out)], 0
        )
        scores = dot(query2, keyed, ((1,), (1,))) * scaling
        shifted = jnp.exp(scores - jnp.max(scores, -1, keepdims=True))
        prob = shifted / jnp.sum(shifted, -1, keepdims=True)
        prob_low = prob.astype(BF)
        dprobs = dot(grad2, valued, ((1,), (1,)))
        row_dot = jnp.sum(prob * dprobs, -1, keepdims=True)
        score_grad = (prob * (dprobs - row_dot) * scaling).astype(BF)
        out2 = dot(prob_low, valued, ((1,), (0,)))
        gq2 = dot(score_grad, keyed, ((1,), (0,)))
        pieces[0].append(jnp.where(first, gq2[:length], gq2[length:]).astype(BF))
        pieces[1].append(dot(score_grad, query2, ((0,), (0,))).astype(BF))
        pieces[2].append(dot(prob_low, grad2, ((0,), (0,))).astype(BF))
        pieces[3].append(jnp.where(first, out2[:length], out2[length:]).astype(BF))
    grads = [jnp.concatenate(piece, 1) for piece in pieces[:3]]
    attended = jnp.concatenate(pieces[3], 1)
    grad_normed = sum(dot(grads[index], w_all[index], ((1,), (0,))) for index in range(3))
    gain_term = jnp.sum(grad_normed * centred, 0, keepdims=True)
    scaled = grad_normed * gain
    branch = inv_std * (
        scaled
        - jnp.mean(scaled, -1, keepdims=True)
        - centred * jnp.mean(scaled * centred, -1, keepdims=True)
    )
    cells = upstream + branch.astype(BF).astype(F32)
    high = gain_term.astype(BF).astype(F32)
    low = gain_term - high
    which = lax.broadcasted_iota(jnp.int32, (tracks, width), 0)
    extra = jnp.where(which == 0, high, jnp.where(which == 1, low, 0.0))
    extra = jnp.broadcast_to(extra[None], (senders, tracks, width))
    cells_ref[...] = jnp.concatenate(
        [cells.reshape(senders, tracks, width), extra], 1
    ).astype(BF)
    for at in range(groups):
        norm_s[at] = normed[:, at * part : (at + 1) * part]
        att_s[at] = attended[:, at * part : (at + 1) * part]
    for step in range(groups):
        owner = lax.rem(group + step, groups)
        norm_part, att_part = norm_s[owner], att_s[owner]
        for index in range(4):
            if index < 3:
                block = dot(grads[index], norm_part, ((0,), (0,))).astype(BF)
            else:
                block = dot(up, att_part, ((0,), (0,))).astype(BF)
            block = block.reshape(count, cols, part)
            for to in range(count):
                slot = send_slot(track ^ to, count) if count > 1 else 0
                wg_refs[step][slot, index] = block[to]


def ring(size, step):
    return [(i, (i + step) % size) for i in range(size)]


def swap(array, axis, bits):
    return lax.ppermute(array, axis, [(i, i ^ bits) for i in range(lax.axis_size(axis))])


def join_blocks(parts, offsets, track):
    blocks = jnp.concatenate(parts)
    order = [offset for held in offsets for offset in held]
    where = [order.index(offset) for offset in range(len(order))]
    blocks = jnp.take(blocks, jnp.array(where)[track ^ jnp.arange(len(order))], axis=0)
    count, four, cols, part = blocks.shape
    return blocks.transpose(1, 0, 2, 3).reshape(1, four, count * cols, part)


def cut_blocks(joined, count, track):
    _, four, width, part = joined.shape
    blocks = joined.reshape(four, count, width // count, part).transpose(1, 0, 2, 3)
    slots = [send_slot(offset, count) for offset in range(count)]
    order = [slots.index(slot) for slot in range(count)]
    return jnp.take(blocks, track ^ jnp.array(order), axis=0)


def gather_blocks(block, axis, other):
    count = lax.axis_size(axis)
    held, order, bit = block[None], [0], count // 2
    while bit > 8:
        held = jnp.concatenate([held, swap(held, axis, bit)])
        order = order + [offset ^ bit for offset in order]
        bit //= 2
    far = [bits for bits in (8, 4, 12) if bits < 2 * bit]
    moved = [swap(held, axis, bits) for bits in far]
    moved[0], other = lax.optimization_barrier((moved[0], other))
    held = jnp.concatenate([held] + moved)
    order = order + [offset ^ bits for bits in far for offset in order]
    parts = [swap(held, axis, bits) if bits else held for bits in range(4)]
    return parts, [[offset ^ bits for offset in order] for bits in range(4)], other


def scatter_sum(blocks, axis):
    count = lax.axis_size(axis)
    blocks = blocks.reshape((4, count // 4) + blocks.shape[1:])
    moved = [swap(blocks[bits], axis, bits) for bits in (1, 3, 2)]
    total = blocks[0].astype(F32) + sum(block.astype(F32) for block in moved)
    bit = 4
    while bit < count:
        half = total.shape[0] // 2
        total = total[:half] + swap(total[half:].astype(BF), axis, bit).astype(F32)
        bit *= 2
    return total[0]


def shards(fields, upstream, ln_gain, weights):
    groups, count = lax.axis_size("grp"), lax.axis_size("trk")
    rows_dev, trk_dev, width = fields.shape
    _, part, cols = weights.shape
    cell_count = rows_dev * groups * trk_dev * count
    group, track = lax.axis_index("grp"), lax.axis_index("trk")
    both = jnp.concatenate([fields, upstream], 1)
    parts, offsets, both = gather_blocks(weights.transpose(0, 2, 1), "trk", both)
    row = lax.all_to_all(both, "trk", split_axis=0, concat_axis=0, tiled=True)
    out_shape = (count, 4, cols, part)
    narrow = cols % 16 != 0
    if narrow:
        parts, offsets = [join_blocks(parts, offsets, track)], [[0]]
        out_shape = (1, 4, count * cols, part)
    w_parts = [
        lax.ppermute(held, "grp", ring(groups, k)) if k else held
        for k in range(groups)
        for held in parts
    ]
    place = jnp.stack([group, track]).astype(jnp.int32)
    vmem = pl.BlockSpec(memory_space=pltpu.VMEM)
    *wg, cells = pl.pallas_call(
        functools.partial(row_kernel, groups, offsets),
        out_shape=(jax.ShapeDtypeStruct(out_shape, BF),) * groups
        + (jax.ShapeDtypeStruct((count, 2 * trk_dev, width), BF),),
        in_specs=[pl.BlockSpec(memory_space=pltpu.SMEM), vmem, vmem]
        + [pl.BlockSpec(memory_space=pl.ANY)] * len(w_parts),
        out_specs=(vmem,) * (groups + 1),
        scratch_shapes=[
            pltpu.VMEM((4, width, width), BF),
            pltpu.VMEM((groups, trk_dev * count, part), BF),
            pltpu.VMEM((groups, trk_dev * count, part), BF),
            pltpu.SemaphoreType.DMA((groups * sum(len(held) for held in offsets),)),
        ],
        compiler_params=pltpu.CompilerParams(vmem_limit_bytes=48 * 2**20),
    )(place, row, ln_gain[None], *w_parts)
    if narrow:
        wg = [cut_blocks(blocks, count, track) for blocks in wg]
    back = lax.all_to_all(cells, "trk", split_axis=0, concat_axis=0, tiled=True)
    total = wg[0].astype(F32)
    for k in range(1, groups):
        total = total + lax.ppermute(wg[k], "grp", ring(groups, k)).astype(F32)
    total = scatter_sum(total.astype(BF), "trk")
    grad_fields = back[:, :trk_dev]
    gain_sum = jnp.sum(back[:, trk_dev : trk_dev + 2].astype(F32), (0, 1))
    if groups == 2:
        gain_sum = gain_sum + lax.ppermute(gain_sum, "grp", ring(2, 1))
    else:
        gain_sum = jnp.sum(lax.all_gather(gain_sum, "grp"), 0)
    factor = float(cell_count) ** (-0.5)
    return (grad_fields, total.transpose(0, 2, 1) * factor, gain_sum * factor)


def solution(mesh):
    in_specs = (P("grp", "trk", None), P("grp", "trk", None), P(), P(None, "grp", "trk"))
    out_specs = (P("grp", "trk", None), P(None, "grp", "trk"), P())
    return jax.shard_map(shards, mesh=mesh, in_specs=in_specs, out_specs=out_specs, check_vma=False)
```

```python
import functools

import jax
import jax.numpy as jnp
from jax import lax
from jax.experimental import pallas as pl
from jax.experimental.pallas import tpu as pltpu
from jax.sharding import PartitionSpec as P

HEADS = 8
BF = jnp.bfloat16
F32 = jnp.float32


def dot(a, b, dims):
    return lax.dot_general(a, b, (dims, ((), ())), preferred_element_type=F32)


def send_slot(offset, count):
    slot, bit = offset & 3, 4
    while bit < count:
        slot = slot * 2 + (offset // bit) % 2
        bit *= 2
    return slot


def row_kernel(groups, offsets, place, rows_ref, gain_ref, *refs):
    w_refs, rest = refs[: groups * len(offsets)], refs[groups * len(offsets) :]
    wg_refs, cells_ref, (w_all, norm_s, att_s) = rest[:groups], rest[groups], rest[groups + 1 :]
    group, track = place[0], place[1]
    senders, pair, _ = rows_ref.shape
    tracks = pair // 2
    width = gain_ref.shape[1]
    length = senders * tracks
    count, _, cols, part = wg_refs[0].shape
    for step in range(groups):
        owner = lax.rem(group - step + groups, groups)
        lanes = pl.ds(pl.multiple_of(owner * part, part), part)
        for at, held in enumerate(offsets):
            w_ref = w_refs[step * len(offsets) + at]
            size = w_ref.shape[2]
            for slot, offset in enumerate(held):
                begin = (track ^ offset) * size if len(offsets) > 1 else 0
                rows = pl.ds(pl.multiple_of(begin, size), size)
                for index in range(4):
                    w_all[index, rows, lanes] = w_ref[slot, index]
    both = rows_ref[...].astype(F32)
    values = both[:, :tracks].reshape(length, width)
    upstream = both[:, tracks:].reshape(length, width)
    gain = gain_ref[...]
    row_mean = jnp.mean(values, -1, keepdims=True)
    offset = values - row_mean
    row_var = jnp.mean(offset * offset, -1, keepdims=True)
    inv_std = lax.rsqrt(row_var + 1e-05)
    centred = offset * inv_std
    normed = (centred * gain).astype(BF)
    up = upstream.astype(BF)
    projected = [dot(normed, w_all[index], ((1,), (1,))).astype(BF) for index in range(3)]
    grad_att = dot(up, w_all[3], ((1,), (0,))).astype(BF)
    size = width // HEADS
    scaling = size ** (-0.5)
    span = 2 * size
    lane = lax.broadcasted_iota(jnp.int32, (length, span), 1)
    first = lane < size
    pieces = [[], [], [], []]
    for at in range(0, width, span):
        query, keyed, valued = [member[:, at : at + span] for member in projected]
        grad_out = grad_att[:, at : at + span]
        zero = jnp.zeros_like(query)
        query2 = jnp.concatenate([jnp.where(first, query, zero), jnp.where(first, zero, query)], 0)
        grad2 = jnp.concatenate(
            [jnp.where(first, grad_out, zero), jnp.where(first, zero, grad_out)], 0
        )
        scores = dot(query2, keyed, ((1,), (1,))) * scaling
        shifted = jnp.exp(scores - jnp.max(scores, -1, keepdims=True))
        prob = shifted / jnp.sum(shifted, -1, keepdims=True)
        prob_low = prob.astype(BF)
        dprobs = dot(grad2, valued, ((1,), (1,)))
        row_dot = jnp.sum(prob * dprobs, -1, keepdims=True)
        score_grad = (prob * (dprobs - row_dot) * scaling).astype(BF)
        out2 = dot(prob_low, valued, ((1,), (0,)))
        gq2 = dot(score_grad, keyed, ((1,), (0,)))
        pieces[0].append(jnp.where(first, gq2[:length], gq2[length:]).astype(BF))
        pieces[1].append(dot(score_grad, query2, ((0,), (0,))).astype(BF))
        pieces[2].append(dot(prob_low, grad2, ((0,), (0,))).astype(BF))
        pieces[3].append(jnp.where(first, out2[:length], out2[length:]).astype(BF))
    grads = [jnp.concatenate(piece, 1) for piece in pieces[:3]]
    attended = jnp.concatenate(pieces[3], 1)
    grad_normed = sum(dot(grads[index], w_all[index], ((1,), (0,))) for index in range(3))
    gain_term = jnp.sum(grad_normed * centred, 0, keepdims=True)
    scaled = grad_normed * gain
    branch = inv_std * (
        scaled
        - jnp.mean(scaled, -1, keepdims=True)
        - centred * jnp.mean(scaled * centred, -1, keepdims=True)
    )
    cells = upstream + branch.astype(BF).astype(F32)
    high = gain_term.astype(BF).astype(F32)
    terms = jnp.concatenate([high, gain_term - high], 1)
    lanes = 2 * width // tracks
    terms = jnp.concatenate([terms[:, at * lanes : (at + 1) * lanes] for at in range(tracks)], 0)
    terms = jnp.broadcast_to(terms[None], (senders, tracks, lanes)).reshape(length, lanes)
    cells_ref[...] = jnp.concatenate([cells, terms], 1).astype(BF)
    for at in range(groups):
        norm_s[at] = normed[:, at * part : (at + 1) * part]
        att_s[at] = attended[:, at * part : (at + 1) * part]
    for step in range(groups):
        owner = lax.rem(group + step, groups)
        norm_part, att_part = norm_s[owner], att_s[owner]
        for index in range(4):
            if index < 3:
                block = dot(grads[index], norm_part, ((0,), (0,))).astype(BF)
            else:
                block = dot(up, att_part, ((0,), (0,))).astype(BF)
            block = block.reshape(count, cols, part)
            for to in range(count):
                slot = send_slot(track ^ to, count) if count > 1 else 0
                wg_refs[step][slot, index] = block[to]


def ring(size, step):
    return [(i, (i + step) % size) for i in range(size)]


def swap(array, axis, bits):
    return lax.ppermute(array, axis, [(i, i ^ bits) for i in range(lax.axis_size(axis))])


def join_blocks(parts, offsets, track):
    blocks = jnp.concatenate(parts)
    order = [offset for held in offsets for offset in held]
    where = [order.index(offset) for offset in range(len(order))]
    blocks = jnp.take(blocks, jnp.array(where)[track ^ jnp.arange(len(order))], axis=0)
    count, four, cols, part = blocks.shape
    return blocks.transpose(1, 0, 2, 3).reshape(1, four, count * cols, part)


def cut_blocks(joined, count, track):
    _, four, width, part = joined.shape
    blocks = joined.reshape(four, count, width // count, part).transpose(1, 0, 2, 3)
    slots = [send_slot(offset, count) for offset in range(count)]
    order = [slots.index(slot) for slot in range(count)]
    return jnp.take(blocks, track ^ jnp.array(order), axis=0)


def gather_blocks(block, axis, other):
    count = lax.axis_size(axis)
    held, order, bit = block[None], [0], count // 2
    while bit > 8:
        held = jnp.concatenate([held, swap(held, axis, bit)])
        order = order + [offset ^ bit for offset in order]
        bit //= 2
    far = [bits for bits in (8, 4, 12) if bits < 2 * bit]
    moved = [swap(held, axis, bits) for bits in far]
    moved[0], other = lax.optimization_barrier((moved[0], other))
    held = jnp.concatenate([held] + moved)
    order = order + [offset ^ bits for bits in far for offset in order]
    parts = [swap(held, axis, bits) if bits else held for bits in range(4)]
    return parts, [[offset ^ bits for offset in order] for bits in range(4)], other


def scatter_sum(blocks, axis):
    count = lax.axis_size(axis)
    blocks = blocks.reshape((4, count // 4) + blocks.shape[1:])
    moved = [swap(blocks[bits], axis, bits) for bits in (1, 3, 2)]
    total = blocks[0].astype(F32) + sum(block.astype(F32) for block in moved)
    bit = 4
    while total.shape[0] > 4:
        half = total.shape[0] // 2
        total = total[:half] + swap(total[half:].astype(BF), axis, bit).astype(F32)
        bit *= 2
    low = total.astype(BF)
    return [total[0]] + [swap(low[at], axis, bits * bit) for at, bits in ((1, 2), (2, 1), (3, 3))]


def shards(fields, upstream, ln_gain, weights):
    groups, count = lax.axis_size("grp"), lax.axis_size("trk")
    rows_dev, trk_dev, width = fields.shape
    _, part, cols = weights.shape
    cell_count = rows_dev * groups * trk_dev * count
    group, track = lax.axis_index("grp"), lax.axis_index("trk")
    both = jnp.concatenate([fields, upstream], 1)
    parts, offsets, both = gather_blocks(weights.transpose(0, 2, 1), "trk", both)
    row = lax.all_to_all(both, "trk", split_axis=0, concat_axis=0, tiled=True)
    out_shape = (count, 4, cols, part)
    narrow = cols % 16 != 0
    if narrow:
        parts, offsets = [join_blocks(parts, offsets, track)], [[0]]
        out_shape = (1, 4, count * cols, part)
    w_parts = [
        lax.ppermute(held, "grp", ring(groups, k)) if k else held
        for k in range(groups)
        for held in parts
    ]
    place = jnp.stack([group, track]).astype(jnp.int32)
    vmem = pl.BlockSpec(memory_space=pltpu.VMEM)
    *wg, cells = pl.pallas_call(
        functools.partial(row_kernel, groups, offsets),
        out_shape=(jax.ShapeDtypeStruct(out_shape, BF),) * groups
        + (jax.ShapeDtypeStruct((count * trk_dev, width + 2 * width // trk_dev), BF),),
        in_specs=[pl.BlockSpec(memory_space=pltpu.SMEM)] + [vmem] * (2 + len(w_parts)),
        out_specs=(vmem,) * (groups + 1),
        scratch_shapes=[
            pltpu.VMEM((4, width, width), BF),
            pltpu.VMEM((groups, trk_dev * count, part), BF),
            pltpu.VMEM((groups, trk_dev * count, part), BF),
        ],
        compiler_params=pltpu.CompilerParams(vmem_limit_bytes=48 * 2**20),
    )(place, row, ln_gain[None], *w_parts)
    if narrow:
        wg = [cut_blocks(blocks, count, track) for blocks in wg]
    back = lax.all_to_all(cells, "trk", split_axis=0, concat_axis=0, tiled=True)
    total = wg[0].astype(F32)
    for k in range(1, groups):
        total = total + lax.ppermute(wg[k], "grp", ring(groups, k)).astype(F32)
    terms = scatter_sum(total.astype(BF), "trk")
    terms[3], back = lax.optimization_barrier((terms[3], back))
    grad_fields = back[:, :width].reshape(count, trk_dev, width)
    gain_sum = jnp.sum(back[:, width:].astype(F32).reshape(count, 2, width), (0, 1))
    if groups == 2:
        gain_sum = gain_sum + lax.ppermute(gain_sum, "grp", ring(2, 1))
    else:
        gain_sum = jnp.sum(lax.all_gather(gain_sum, "grp"), 0)
    terms[1], terms[2], grad_fields, gain_sum = lax.optimization_barrier((terms[1], terms[2], grad_fields, gain_sum))
    total = sum(term.astype(F32) for term in terms)
    factor = float(cell_count) ** (-0.5)
    return (grad_fields, total.transpose(0, 2, 1) * factor, gain_sum * factor)


def solution(mesh):
    in_specs = (P("grp", "trk", None), P("grp", "trk", None), P(), P(None, "grp", "trk"))
    out_specs = (P("grp", "trk", None), P(None, "grp", "trk"), P())
    return jax.shard_map(shards, mesh=mesh, in_specs=in_specs, out_specs=out_specs, check_vma=False)
```

```python
import functools

import jax
import jax.numpy as jnp
from jax import lax
from jax.experimental import pallas as pl
from jax.experimental.pallas import tpu as pltpu
from jax.sharding import PartitionSpec as P

HEADS = 8
BF = jnp.bfloat16
F32 = jnp.float32


def dot(a, b, dims):
    return lax.dot_general(a, b, (dims, ((), ())), preferred_element_type=F32)


def send_slot(offset, count):
    slot, bit = offset & 3, 4
    while bit < count:
        slot = slot * 2 + (offset // bit) % 2
        bit *= 2
    return slot


def join_weights(groups, offsets, group, track, w_refs, w_all):
    for step in range(groups):
        for at, held in enumerate(offsets):
            w_ref = w_refs[step * len(offsets) + at]
            _, _, size, part = w_ref.shape
            owner = lax.rem(group - step + groups, groups)
            lanes = pl.ds(pl.multiple_of(owner * part, part), part)
            for slot, offset in enumerate(held):
                begin = (track ^ offset) * size if len(offsets) > 1 else 0
                rows = pl.ds(pl.multiple_of(begin, size), size)
                for index in range(4):
                    w_all[index, rows, lanes] = w_ref[slot, index]


def read_row(rows_ref):
    senders, pair, width = rows_ref.shape
    tracks = pair // 2
    both = rows_ref[...].astype(F32)
    return [both[:, at : at + tracks].reshape(senders * tracks, width) for at in (0, tracks)]


def normalize(values, gain):
    row_mean = jnp.mean(values, -1, keepdims=True)
    offset = values - row_mean
    row_var = jnp.mean(offset * offset, -1, keepdims=True)
    inv_std = lax.rsqrt(row_var + 1e-05)
    centred = offset * inv_std
    return (centred * gain).astype(BF), centred, inv_std


def write_grads(track, wg_ref, grads, up, norm_part, att_part):
    count, _, cols, part = wg_ref.shape
    for index in range(4):
        if index < 3:
            block = dot(grads[index], norm_part, ((0,), (0,))).astype(BF)
        else:
            block = dot(up, att_part, ((0,), (0,))).astype(BF)
        block = block.reshape(count, cols, part)
        for to in range(count):
            slot = send_slot(track ^ to, count) if count > 1 else 0
            wg_ref[slot, index] = block[to]


def pick(array, group, groups, scratch):
    part = array.shape[1] // groups
    for at in range(groups):
        scratch[at] = array[:, at * part : (at + 1) * part]
    return scratch[group]


def attend_kernel(groups, offsets, place, rows_ref, gain_ref, *refs):
    held = groups * len(offsets)
    w_refs, wg_refs, refs = refs[:held], refs[held : held + groups - 1], refs[held + groups - 1 :]
    grads_ref, att_ref, w_all, same_gain_ref, norm_s, att_s = refs
    group, track = place[0], place[1]
    join_weights(groups, offsets, group, track, w_refs, w_all)
    values, upstream = read_row(rows_ref)
    length, width = values.shape
    normed, _, _ = normalize(values, gain_ref[...][:1])
    up = upstream.astype(BF)
    projected = [dot(normed, w_all[index], ((1,), (1,))).astype(BF) for index in range(3)]
    grad_att = dot(up, w_all[3], ((1,), (0,))).astype(BF)
    size = width // HEADS
    scaling = size ** (-0.5)
    span = 2 * size
    lane = lax.broadcasted_iota(jnp.int32, (length, span), 1)
    first = lane < size
    pieces = [[], [], [], []]
    for at in range(0, width, span):
        query, keyed, valued = [member[:, at : at + span] for member in projected]
        grad_out = grad_att[:, at : at + span]
        zero = jnp.zeros_like(query)
        query2 = jnp.concatenate([jnp.where(first, query, zero), jnp.where(first, zero, query)], 0)
        grad2 = jnp.concatenate(
            [jnp.where(first, grad_out, zero), jnp.where(first, zero, grad_out)], 0
        )
        scores = dot(query2, keyed, ((1,), (1,))) * scaling
        shifted = jnp.exp(scores - jnp.max(scores, -1, keepdims=True))
        prob = shifted / jnp.sum(shifted, -1, keepdims=True)
        prob_low = prob.astype(BF)
        dprobs = dot(grad2, valued, ((1,), (1,)))
        row_dot = jnp.sum(prob * dprobs, -1, keepdims=True)
        score_grad = (prob * (dprobs - row_dot) * scaling).astype(BF)
        out2 = dot(prob_low, valued, ((1,), (0,)))
        gq2 = dot(score_grad, keyed, ((1,), (0,)))
        pieces[0].append(jnp.where(first, gq2[:length], gq2[length:]).astype(BF))
        pieces[1].append(dot(score_grad, query2, ((0,), (0,))).astype(BF))
        pieces[2].append(dot(prob_low, grad2, ((0,), (0,))).astype(BF))
        pieces[3].append(jnp.where(first, out2[:length], out2[length:]).astype(BF))
    grads = [jnp.concatenate(piece, 1) for piece in pieces[:3]]
    attended = jnp.concatenate(pieces[3], 1)
    for step in range(1, groups):
        owner = lax.rem(group + step, groups)
        write_grads(
            track,
            wg_refs[step - 1],
            grads,
            up,
            pick(normed, owner, groups, norm_s),
            pick(attended, owner, groups, att_s),
        )
    for index in range(3):
        grads_ref[index] = grads[index]
    att_ref[...] = attended
    same_gain_ref[...] = gain_ref[...][:1]


def cells_kernel(groups, place, rows_ref, gain_ref, w_all, grads_ref, att_ref, wg_ref, cells_ref, norm_s, att_s):
    group, track = place[0], place[1]
    values, upstream = read_row(rows_ref)
    senders, tracks = rows_ref.shape[0], rows_ref.shape[1] // 2
    length, width = values.shape
    gain = gain_ref[...]
    normed, centred, inv_std = normalize(values, gain)
    grads = [grads_ref[index] for index in range(3)]
    grad_normed = sum(dot(grads[index], w_all[index], ((1,), (0,))) for index in range(3))
    gain_term = jnp.sum(grad_normed * centred, 0, keepdims=True)
    scaled = grad_normed * gain
    branch = inv_std * (
        scaled
        - jnp.mean(scaled, -1, keepdims=True)
        - centred * jnp.mean(scaled * centred, -1, keepdims=True)
    )
    cells = upstream + branch.astype(BF).astype(F32)
    high = gain_term.astype(BF).astype(F32)
    terms = jnp.concatenate([high, gain_term - high], 1)
    lanes = 2 * width // tracks
    terms = jnp.concatenate([terms[:, at * lanes : (at + 1) * lanes] for at in range(tracks)], 0)
    terms = jnp.broadcast_to(terms[None], (senders, tracks, lanes)).reshape(length, lanes)
    cells_ref[...] = jnp.concatenate([cells, terms], 1).astype(BF)
    write_grads(
        track,
        wg_ref,
        grads,
        upstream.astype(BF),
        pick(normed, group, groups, norm_s),
        pick(att_ref[...], group, groups, att_s),
    )


def ring(size, step):
    return [(i, (i + step) % size) for i in range(size)]


def swap(array, axis, bits):
    return lax.ppermute(array, axis, [(i, i ^ bits) for i in range(lax.axis_size(axis))])


def join_blocks(parts, offsets, track):
    blocks = jnp.concatenate(parts)
    order = [offset for held in offsets for offset in held]
    where = [order.index(offset) for offset in range(len(order))]
    blocks = jnp.take(blocks, jnp.array(where)[track ^ jnp.arange(len(order))], axis=0)
    count, four, cols, part = blocks.shape
    return blocks.transpose(1, 0, 2, 3).reshape(1, four, count * cols, part)


def cut_blocks(joined, count, track):
    _, four, width, part = joined.shape
    blocks = joined.reshape(four, count, width // count, part).transpose(1, 0, 2, 3)
    slots = [send_slot(offset, count) for offset in range(count)]
    order = [slots.index(slot) for slot in range(count)]
    return jnp.take(blocks, track ^ jnp.array(order), axis=0)


def gather_blocks(block, axis, other):
    count = lax.axis_size(axis)
    held, order, bit = block[None], [0], count // 2
    while bit > 8:
        held = jnp.concatenate([held, swap(held, axis, bit)])
        order = order + [offset ^ bit for offset in order]
        bit //= 2
    far = [bits for bits in (8, 4, 12) if bits < 2 * bit]
    moved = [swap(held, axis, bits) for bits in far]
    moved[0], other = lax.optimization_barrier((moved[0], other))
    held = jnp.concatenate([held] + moved)
    order = order + [offset ^ bits for bits in far for offset in order]
    parts = [swap(held, axis, bits) if bits else held for bits in range(4)]
    return parts, [[offset ^ bits for offset in order] for bits in range(4)], other


def scatter_sum(blocks, axis):
    count = lax.axis_size(axis)
    blocks = blocks.reshape((4, count // 4) + blocks.shape[1:])
    moved = [swap(blocks[bits], axis, bits) for bits in (1, 3, 2)]
    total = blocks[0].astype(F32) + sum(block.astype(F32) for block in moved)
    bit = 4
    while total.shape[0] > 4:
        half = total.shape[0] // 2
        total = total[:half] + swap(total[half:].astype(BF), axis, bit).astype(F32)
        bit *= 2
    low = total.astype(BF)
    return [total[0]] + [swap(low[at], axis, bits * bit) for at, bits in ((1, 2), (2, 1), (3, 3))]


def shards(fields, upstream, ln_gain, weights):
    groups, count = lax.axis_size("grp"), lax.axis_size("trk")
    rows_dev, trk_dev, width = fields.shape
    _, part, cols = weights.shape
    cell_count = rows_dev * groups * trk_dev * count
    group, track = lax.axis_index("grp"), lax.axis_index("trk")
    both = jnp.concatenate([fields, upstream], 1)
    gain = jnp.broadcast_to(ln_gain, (8, width))
    place = jnp.stack([group, track]).astype(jnp.int32)
    place, gain, both = lax.optimization_barrier((place, gain, both))
    parts, offsets, both = gather_blocks(weights.transpose(0, 2, 1), "trk", both)
    row = lax.all_to_all(both, "trk", split_axis=0, concat_axis=0, tiled=True)
    out_shape = (count, 4, cols, part)
    narrow = cols % 16 != 0
    if narrow:
        parts, offsets = [join_blocks(parts, offsets, track)], [[0]]
        out_shape = (1, 4, count * cols, part)
    w_parts = [
        lax.ppermute(held, "grp", ring(groups, k)) if k else held
        for k in range(groups)
        for held in parts
    ]
    vmem = pl.BlockSpec(memory_space=pltpu.VMEM)
    smem = pl.BlockSpec(memory_space=pltpu.SMEM)
    length = trk_dev * count
    wg_shape = jax.ShapeDtypeStruct(out_shape, BF)
    scratch = [pltpu.VMEM((groups, length, part), BF)] * 2
    *wg, grads, attended, w_all, gain = pl.pallas_call(
        functools.partial(attend_kernel, groups, offsets),
        out_shape=(wg_shape,) * (groups - 1)
        + (
            jax.ShapeDtypeStruct((3, length, width), BF),
            jax.ShapeDtypeStruct((length, width), BF),
            jax.ShapeDtypeStruct((4, width, width), BF),
            jax.ShapeDtypeStruct((1, width), F32),
        ),
        in_specs=[smem] + [vmem] * (2 + len(w_parts)),
        out_specs=(vmem,) * (groups + 3),
        scratch_shapes=scratch,
        compiler_params=pltpu.CompilerParams(vmem_limit_bytes=48 * 2**20),
    )(place, row, gain, *w_parts)
    own, cells = pl.pallas_call(
        functools.partial(cells_kernel, groups),
        out_shape=(
            wg_shape,
            jax.ShapeDtypeStruct((length, width + 2 * width // trk_dev), BF),
        ),
        in_specs=[smem] + [vmem] * 5,
        out_specs=(vmem, vmem),
        scratch_shapes=scratch,
        compiler_params=pltpu.CompilerParams(vmem_limit_bytes=48 * 2**20),
        cost_estimate=pl.CostEstimate(
            flops=10 * length * width * width, bytes_accessed=16 * width * width, transcendentals=0
        ),
    )(place, row, gain, w_all, grads, attended)
    wg = [own] + list(wg)
    if narrow:
        wg = [cut_blocks(blocks, count, track) for blocks in wg]
    back = lax.all_to_all(cells, "trk", split_axis=0, concat_axis=0, tiled=True)
    total = wg[0].astype(F32)
    for k in range(1, groups):
        total = total + lax.ppermute(wg[k], "grp", ring(groups, k)).astype(F32)
    terms = scatter_sum(total.astype(BF), "trk")
    terms[3], back = lax.optimization_barrier((terms[3], back))
    grad_fields = back[:, :width].reshape(count, trk_dev, width)
    gain_sum = jnp.sum(back[:, width:].astype(F32).reshape(count, 2, width), (0, 1))
    if groups == 2:
        gain_sum = gain_sum + lax.ppermute(gain_sum, "grp", ring(2, 1))
    else:
        gain_sum = jnp.sum(lax.all_gather(gain_sum, "grp"), 0)
    factor = float(cell_count) ** (-0.5)
    gain_sum = gain_sum * factor
    terms[1], terms[2], grad_fields, gain_sum = lax.optimization_barrier(
        (terms[1], terms[2], grad_fields, gain_sum)
    )
    total = sum(term.astype(F32) for term in terms)
    return (grad_fields, total.transpose(0, 2, 1) * factor, gain_sum)


def solution(mesh):
    in_specs = (P("grp", "trk", None), P("grp", "trk", None), P(), P(None, "grp", "trk"))
    out_specs = (P("grp", "trk", None), P(None, "grp", "trk"), P())
    return jax.shard_map(shards, mesh=mesh, in_specs=in_specs, out_specs=out_specs, check_vma=False)
```

```python
import functools

import jax
import jax.numpy as jnp
from jax import lax
from jax.experimental import pallas as pl
from jax.experimental.pallas import tpu as pltpu
from jax.sharding import PartitionSpec as P

HEADS = 8
BF = jnp.bfloat16
F32 = jnp.float32


def dot(a, b, dims):
    return lax.dot_general(a, b, (dims, ((), ())), preferred_element_type=F32)


def send_slot(offset, count):
    slot, bit = offset & 3, 4
    while bit < count:
        slot = slot * 2 + (offset // bit) % 2
        bit *= 2
    return slot


def join_weights(groups, offsets, group, track, w_refs, w_all):
    for step in range(groups):
        for at, held in enumerate(offsets):
            w_ref = w_refs[step * len(offsets) + at]
            _, _, size, part = w_ref.shape
            owner = lax.rem(group - step + groups, groups)
            lanes = pl.ds(pl.multiple_of(owner * part, part), part)
            for slot, offset in enumerate(held):
                begin = (track ^ offset) * size if len(offsets) > 1 else 0
                rows = pl.ds(pl.multiple_of(begin, size), size)
                for index in range(4):
                    w_all[index, rows, lanes] = w_ref[slot, index]


def read_row(rows_ref):
    senders, pair, width = rows_ref.shape
    tracks = pair // 2
    both = rows_ref[...].astype(F32)
    return [both[:, at : at + tracks].reshape(senders * tracks, width) for at in (0, tracks)]


def normalize(values, gain):
    row_mean = jnp.mean(values, -1, keepdims=True)
    offset = values - row_mean
    row_var = jnp.mean(offset * offset, -1, keepdims=True)
    inv_std = lax.rsqrt(row_var + 1e-05)
    centred = offset * inv_std
    return (centred * gain).astype(BF), centred, inv_std


def write_grads(track, wg_ref, grads, up, norm_part, att_part):
    count, _, cols, part = wg_ref.shape
    for index in range(4):
        if index < 3:
            block = dot(grads[index], norm_part, ((0,), (0,))).astype(BF)
        else:
            block = dot(up, att_part, ((0,), (0,))).astype(BF)
        block = block.reshape(count, cols, part)
        for to in range(count):
            slot = send_slot(track ^ to, count) if count > 1 else 0
            wg_ref[slot, index] = block[to]


def pick(array, group, groups, scratch):
    part = array.shape[1] // groups
    for at in range(groups):
        scratch[at] = array[:, at * part : (at + 1) * part]
    return scratch[group]


def attend_kernel(groups, offsets, place, rows_ref, gain_ref, *refs):
    held = groups * len(offsets)
    w_refs, wg_refs, refs = refs[:held], refs[held : held + groups - 1], refs[held + groups - 1 :]
    grads_ref, att_ref, w_all, same_gain_ref, norm_s, att_s = refs
    group, track = place[0], place[1]
    join_weights(groups, offsets, group, track, w_refs, w_all)
    values, upstream = read_row(rows_ref)
    length, width = values.shape
    normed, _, _ = normalize(values, gain_ref[...][:1])
    up = upstream.astype(BF)
    projected = [dot(normed, w_all[index], ((1,), (1,))).astype(BF) for index in range(3)]
    grad_att = dot(up, w_all[3], ((1,), (0,))).astype(BF)
    size = width // HEADS
    scaling = size ** (-0.5)
    span = 2 * size
    lane = lax.broadcasted_iota(jnp.int32, (length, span), 1)
    first = lane < size
    spans = [slice(at, at + span) for at in range(0, width, span)]
    query, keyed, valued = [[member[:, at] for at in spans] for member in projected]
    grad_out = [grad_att[:, at] for at in spans]
    zero = jnp.zeros((length, span), BF)

    def apart(member):
        return jnp.concatenate([jnp.where(first, member, zero), jnp.where(first, zero, member)], 0)

    def together(member):
        return jnp.where(first, member[:length], member[length:]).astype(BF)

    query2, grad2 = [apart(m) for m in query], [apart(m) for m in grad_out]
    scores = [dot(k, q, ((1,), (1,))) * scaling for k, q in zip(keyed, query2)]
    dprobs = [dot(v, g, ((1,), (1,))) for v, g in zip(valued, grad2)]
    shifted = [jnp.exp(s - jnp.max(s, 0, keepdims=True)) for s in scores]
    prob = [s * (1.0 / jnp.sum(s, 0, keepdims=True)) for s in shifted]
    prob_low = [p.astype(BF) for p in prob]
    row_dot = [jnp.sum(p * d, 0, keepdims=True) for p, d in zip(prob, dprobs)]
    score_grad = [
        (p * (d - r) * scaling).astype(BF) for p, d, r in zip(prob, dprobs, row_dot)
    ]
    pieces = [
        [together(dot(s, k, ((0,), (0,)))) for s, k in zip(score_grad, keyed)],
        [dot(s, q, ((1,), (0,))).astype(BF) for s, q in zip(score_grad, query2)],
        [dot(p, g, ((1,), (0,))).astype(BF) for p, g in zip(prob_low, grad2)],
        [together(dot(p, v, ((0,), (0,)))) for p, v in zip(prob_low, valued)],
    ]
    grads = [jnp.concatenate(piece, 1) for piece in pieces[:3]]
    attended = jnp.concatenate(pieces[3], 1)
    for step in range(1, groups):
        owner = lax.rem(group + step, groups)
        write_grads(
            track,
            wg_refs[step - 1],
            grads,
            up,
            pick(normed, owner, groups, norm_s),
            pick(attended, owner, groups, att_s),
        )
    for index in range(3):
        grads_ref[index] = grads[index]
    att_ref[...] = attended
    same_gain_ref[...] = gain_ref[...][:1]


def cells_kernel(groups, place, rows_ref, gain_ref, w_all, grads_ref, att_ref, wg_ref, cells_ref, norm_s, att_s):
    group, track = place[0], place[1]
    values, upstream = read_row(rows_ref)
    senders, tracks = rows_ref.shape[0], rows_ref.shape[1] // 2
    length, width = values.shape
    gain = gain_ref[...]
    normed, centred, inv_std = normalize(values, gain)
    grads = [grads_ref[index] for index in range(3)]
    grad_normed = sum(dot(grads[index], w_all[index], ((1,), (0,))) for index in range(3))
    gain_term = jnp.sum(grad_normed * centred, 0, keepdims=True)
    scaled = grad_normed * gain
    branch = inv_std * (
        scaled
        - jnp.mean(scaled, -1, keepdims=True)
        - centred * jnp.mean(scaled * centred, -1, keepdims=True)
    )
    cells = upstream + branch.astype(BF).astype(F32)
    high = gain_term.astype(BF).astype(F32)
    terms = jnp.concatenate([high, gain_term - high], 1)
    lanes = 2 * width // tracks
    terms = jnp.concatenate([terms[:, at * lanes : (at + 1) * lanes] for at in range(tracks)], 0)
    terms = jnp.broadcast_to(terms[None], (senders, tracks, lanes)).reshape(length, lanes)
    cells_ref[...] = jnp.concatenate([cells, terms], 1).astype(BF)
    write_grads(
        track,
        wg_ref,
        grads,
        upstream.astype(BF),
        pick(normed, group, groups, norm_s),
        pick(att_ref[...], group, groups, att_s),
    )


def ring(size, step):
    return [(i, (i + step) % size) for i in range(size)]


def swap(array, axis, bits):
    return lax.ppermute(array, axis, [(i, i ^ bits) for i in range(lax.axis_size(axis))])


def join_blocks(parts, offsets, track):
    blocks = jnp.concatenate(parts)
    order = [offset for held in offsets for offset in held]
    where = [order.index(offset) for offset in range(len(order))]
    blocks = jnp.take(blocks, jnp.array(where)[track ^ jnp.arange(len(order))], axis=0)
    count, four, cols, part = blocks.shape
    return blocks.transpose(1, 0, 2, 3).reshape(1, four, count * cols, part)


def cut_blocks(joined, count, track):
    _, four, width, part = joined.shape
    blocks = joined.reshape(four, count, width // count, part).transpose(1, 0, 2, 3)
    slots = [send_slot(offset, count) for offset in range(count)]
    order = [slots.index(slot) for slot in range(count)]
    return jnp.take(blocks, track ^ jnp.array(order), axis=0)


def stack_blocks(parts):
    def kernel(*refs):
        at = 0
        for ref in refs[:-1]:
            refs[-1][at : at + ref.shape[0]] = ref[...]
            at += ref.shape[0]

    vmem = pl.BlockSpec(memory_space=pltpu.VMEM)
    shape = (sum(part.shape[0] for part in parts),) + parts[0].shape[1:]
    return pl.pallas_call(
        kernel,
        out_shape=jax.ShapeDtypeStruct(shape, BF),
        in_specs=[vmem] * len(parts),
        out_specs=vmem,
        compiler_params=pltpu.CompilerParams(vmem_limit_bytes=16 * 2**20),
    )(*parts)


def gather_blocks(block, axis, other):
    count = lax.axis_size(axis)
    held, order, bit = block[None], [0], count // 2
    while bit > 8:
        held = jnp.concatenate([held, swap(held, axis, bit)])
        order = order + [offset ^ bit for offset in order]
        bit //= 2
    far = [bits for bits in (8, 4, 12) if bits < 2 * bit]
    moved = [swap(held, axis, bits) for bits in far]
    held, other = lax.optimization_barrier((stack_blocks([held]), other))
    moved[0], other = lax.optimization_barrier((moved[0], other))
    held = stack_blocks([held] + moved)
    order = order + [offset ^ bits for bits in far for offset in order]
    parts = [swap(held, axis, bits) if bits else held for bits in range(4)]
    return parts, [[offset ^ bits for offset in order] for bits in range(4)], other


def scatter_sum(blocks, axis):
    count = lax.axis_size(axis)
    blocks = blocks.reshape((4, count // 4) + blocks.shape[1:])
    moved = [swap(blocks[bits], axis, bits) for bits in (1, 3, 2)]
    total = blocks[0].astype(F32) + sum(block.astype(F32) for block in moved)
    bit = 4
    while total.shape[0] > 4:
        half = total.shape[0] // 2
        total = total[:half] + swap(total[half:].astype(BF), axis, bit).astype(F32)
        bit *= 2
    low = total.astype(BF)
    return [total[0]] + [swap(low[at], axis, bits * bit) for at, bits in ((1, 2), (2, 1), (3, 3))]


def shards(fields, upstream, ln_gain, weights):
    groups, count = lax.axis_size("grp"), lax.axis_size("trk")
    rows_dev, trk_dev, width = fields.shape
    _, part, cols = weights.shape
    cell_count = rows_dev * groups * trk_dev * count
    group, track = lax.axis_index("grp"), lax.axis_index("trk")
    both = jnp.concatenate([fields, upstream], 1)
    gain = jnp.broadcast_to(ln_gain, (8, width))
    place = jnp.stack([group, track]).astype(jnp.int32)
    place, gain, both = lax.optimization_barrier((place, gain, both))
    parts, offsets, both = gather_blocks(weights.transpose(0, 2, 1), "trk", both)
    row = lax.all_to_all(both, "trk", split_axis=0, concat_axis=0, tiled=True)
    out_shape = (count, 4, cols, part)
    narrow = cols % 16 != 0
    if narrow:
        parts, offsets = [join_blocks(parts, offsets, track)], [[0]]
        out_shape = (1, 4, count * cols, part)
    w_parts = [
        lax.ppermute(held, "grp", ring(groups, k)) if k else held
        for k in range(groups)
        for held in parts
    ]
    vmem = pl.BlockSpec(memory_space=pltpu.VMEM)
    smem = pl.BlockSpec(memory_space=pltpu.SMEM)
    length = trk_dev * count
    wg_shape = jax.ShapeDtypeStruct(out_shape, BF)
    scratch = [pltpu.VMEM((groups, length, part), BF)] * 2
    *wg, grads, attended, w_all, gain = pl.pallas_call(
        functools.partial(attend_kernel, groups, offsets),
        out_shape=(wg_shape,) * (groups - 1)
        + (
            jax.ShapeDtypeStruct((3, length, width), BF),
            jax.ShapeDtypeStruct((length, width), BF),
            jax.ShapeDtypeStruct((4, width, width), BF),
            jax.ShapeDtypeStruct((1, width), F32),
        ),
        in_specs=[smem] + [vmem] * (2 + len(w_parts)),
        out_specs=(vmem,) * (groups + 3),
        scratch_shapes=scratch,
        compiler_params=pltpu.CompilerParams(vmem_limit_bytes=48 * 2**20),
    )(place, row, gain, *w_parts)
    own, cells = pl.pallas_call(
        functools.partial(cells_kernel, groups),
        out_shape=(
            wg_shape,
            jax.ShapeDtypeStruct((length, width + 2 * width // trk_dev), BF),
        ),
        in_specs=[smem] + [vmem] * 5,
        out_specs=(vmem, vmem),
        scratch_shapes=scratch,
        compiler_params=pltpu.CompilerParams(vmem_limit_bytes=48 * 2**20),
        cost_estimate=pl.CostEstimate(
            flops=10 * length * width * width, bytes_accessed=16 * width * width, transcendentals=0
        ),
    )(place, row, gain, w_all, grads, attended)
    wg = [own] + list(wg)
    if narrow:
        wg = [cut_blocks(blocks, count, track) for blocks in wg]
    back = lax.all_to_all(cells, "trk", split_axis=0, concat_axis=0, tiled=True)
    total = wg[0].astype(F32)
    for k in range(1, groups):
        total = total + lax.ppermute(wg[k], "grp", ring(groups, k)).astype(F32)
    terms = scatter_sum(total.astype(BF), "trk")
    terms[3], back = lax.optimization_barrier((terms[3], back))
    grad_fields = back[:, :width].reshape(count, trk_dev, width)
    gain_sum = jnp.sum(back[:, width:].astype(F32).reshape(count, 2, width), (0, 1))
    if groups == 2:
        gain_sum = gain_sum + lax.ppermute(gain_sum, "grp", ring(2, 1))
    else:
        gain_sum = jnp.sum(lax.all_gather(gain_sum, "grp"), 0)
    factor = float(cell_count) ** (-0.5)
    gain_sum = gain_sum * factor
    terms[1], terms[2], grad_fields, gain_sum = lax.optimization_barrier(
        (terms[1], terms[2], grad_fields, gain_sum)
    )
    total = sum(term.astype(F32) for term in terms)
    return (grad_fields, total.transpose(0, 2, 1) * factor, gain_sum)


def solution(mesh):
    in_specs = (P("grp", "trk", None), P("grp", "trk", None), P(), P(None, "grp", "trk"))
    out_specs = (P("grp", "trk", None), P(None, "grp", "trk"), P())
    return jax.shard_map(shards, mesh=mesh, in_specs=in_specs, out_specs=out_specs, check_vma=False)
```

```python
import functools

import jax
import jax.numpy as jnp
from jax import lax
from jax.experimental import pallas as pl
from jax.experimental.pallas import tpu as pltpu
from jax.sharding import PartitionSpec as P

HEADS = 8
BF = jnp.bfloat16
F32 = jnp.float32


def dot(a, b, dims):
    return lax.dot_general(a, b, (dims, ((), ())), preferred_element_type=F32)


def send_slot(offset, count):
    return (offset & 3) * (count // 4) + offset // 4


def join_weights(groups, offsets, group, track, w_refs, w_all):
    for step in range(groups):
        for at, held in enumerate(offsets):
            w_ref = w_refs[step * len(offsets) + at]
            _, _, size, part = w_ref.shape
            owner = lax.rem(group - step + groups, groups)
            lanes = pl.ds(pl.multiple_of(owner * part, part), part)
            for slot, offset in enumerate(held):
                begin = (track ^ offset) * size if len(offsets) > 1 else 0
                rows = pl.ds(pl.multiple_of(begin, size), size)
                for index in range(4):
                    w_all[index, rows, lanes] = w_ref[slot, index]


def read_row(rows_ref):
    senders, pair, width = rows_ref.shape
    tracks = pair // 2
    both = rows_ref[...].astype(F32)
    return [both[:, at : at + tracks].reshape(senders * tracks, width) for at in (0, tracks)]


def normalize(values, gain):
    row_mean = jnp.mean(values, -1, keepdims=True)
    offset = values - row_mean
    row_var = jnp.mean(offset * offset, -1, keepdims=True)
    inv_std = lax.rsqrt(row_var + 1e-05)
    centred = offset * inv_std
    return (centred * gain).astype(BF), centred, inv_std


def write_grads(track, wg_ref, grads, up, norm_part, att_part):
    count, _, cols, part = wg_ref.shape
    for index in range(4):
        if index < 3:
            block = dot(grads[index], norm_part, ((0,), (0,))).astype(BF)
        else:
            block = dot(up, att_part, ((0,), (0,))).astype(BF)
        block = block.reshape(count, cols, part)
        for to in range(count):
            slot = send_slot(track ^ to, count) if count > 1 else 0
            wg_ref[slot, index] = block[to]


def pick(array, group, groups, scratch):
    part = array.shape[1] // groups
    for at in range(groups):
        scratch[at] = array[:, at * part : (at + 1) * part]
    return scratch[group]


def attend_kernel(groups, offsets, place, rows_ref, gain_ref, *refs):
    held = groups * len(offsets)
    w_refs, wg_refs, refs = refs[:held], refs[held : held + groups - 1], refs[held + groups - 1 :]
    grads_ref, att_ref, w_all, same_gain_ref, norm_s, att_s = refs
    group, track = place[0], place[1]
    join_weights(groups, offsets, group, track, w_refs, w_all)
    values, upstream = read_row(rows_ref)
    length, width = values.shape
    normed, _, _ = normalize(values, gain_ref[...][:1])
    up = upstream.astype(BF)
    projected = [dot(normed, w_all[index], ((1,), (1,))).astype(BF) for index in range(3)]
    grad_att = dot(up, w_all[3], ((1,), (0,))).astype(BF)
    size = width // HEADS
    scaling = size ** (-0.5)
    span = 2 * size
    lane = lax.broadcasted_iota(jnp.int32, (length, span), 1)
    first = lane < size
    spans = [slice(at, at + span) for at in range(0, width, span)]
    query, keyed, valued = [[member[:, at] for at in spans] for member in projected]
    grad_out = [grad_att[:, at] for at in spans]
    zero = jnp.zeros((length, span), BF)

    def apart(member):
        return jnp.concatenate([jnp.where(first, member, zero), jnp.where(first, zero, member)], 0)

    def together(member):
        return jnp.where(first, member[:length], member[length:]).astype(BF)

    query2, grad2 = [apart(m) for m in query], [apart(m) for m in grad_out]
    scores = [dot(k, q, ((1,), (1,))) * scaling for k, q in zip(keyed, query2)]
    dprobs = [dot(v, g, ((1,), (1,))) for v, g in zip(valued, grad2)]
    shifted = [jnp.exp(s - jnp.max(s, 0, keepdims=True)) for s in scores]
    prob = [s * (1.0 / jnp.sum(s, 0, keepdims=True)) for s in shifted]
    prob_low = [p.astype(BF) for p in prob]
    row_dot = [jnp.sum(p * d, 0, keepdims=True) for p, d in zip(prob, dprobs)]
    score_grad = [
        (p * (d - r) * scaling).astype(BF) for p, d, r in zip(prob, dprobs, row_dot)
    ]
    pieces = [
        [together(dot(s, k, ((0,), (0,)))) for s, k in zip(score_grad, keyed)],
        [dot(s, q, ((1,), (0,))).astype(BF) for s, q in zip(score_grad, query2)],
        [dot(p, g, ((1,), (0,))).astype(BF) for p, g in zip(prob_low, grad2)],
        [together(dot(p, v, ((0,), (0,)))) for p, v in zip(prob_low, valued)],
    ]
    grads = [jnp.concatenate(piece, 1) for piece in pieces[:3]]
    attended = jnp.concatenate(pieces[3], 1)
    for step in range(1, groups):
        owner = lax.rem(group + step, groups)
        write_grads(
            track,
            wg_refs[step - 1],
            grads,
            up,
            pick(normed, owner, groups, norm_s),
            pick(attended, owner, groups, att_s),
        )
    for index in range(3):
        grads_ref[index] = grads[index]
    att_ref[...] = attended
    same_gain_ref[...] = gain_ref[...][:1]


def cells_kernel(groups, place, rows_ref, gain_ref, w_all, grads_ref, att_ref, wg_ref, cells_ref, norm_s, att_s):
    group, track = place[0], place[1]
    values, upstream = read_row(rows_ref)
    senders, tracks = rows_ref.shape[0], rows_ref.shape[1] // 2
    length, width = values.shape
    gain = gain_ref[...]
    normed, centred, inv_std = normalize(values, gain)
    grads = [grads_ref[index] for index in range(3)]
    grad_normed = sum(dot(grads[index], w_all[index], ((1,), (0,))) for index in range(3))
    gain_term = jnp.sum(grad_normed * centred, 0, keepdims=True)
    scaled = grad_normed * gain
    branch = inv_std * (
        scaled
        - jnp.mean(scaled, -1, keepdims=True)
        - centred * jnp.mean(scaled * centred, -1, keepdims=True)
    )
    cells = upstream + branch.astype(BF).astype(F32)
    high = gain_term.astype(BF).astype(F32)
    terms = jnp.concatenate([high, gain_term - high], 1)
    lanes = 2 * width // tracks
    terms = jnp.concatenate([terms[:, at * lanes : (at + 1) * lanes] for at in range(tracks)], 0)
    terms = jnp.broadcast_to(terms[None], (senders, tracks, lanes)).reshape(length, lanes)
    cells_ref[...] = jnp.concatenate([cells, terms], 1).astype(BF)
    write_grads(
        track,
        wg_ref,
        grads,
        upstream.astype(BF),
        pick(normed, group, groups, norm_s),
        pick(att_ref[...], group, groups, att_s),
    )


def ring(size, step):
    return [(i, (i + step) % size) for i in range(size)]


def swap(array, axis, bits):
    return lax.ppermute(array, axis, [(i, i ^ bits) for i in range(lax.axis_size(axis))])


def join_blocks(parts, offsets, track):
    blocks = jnp.concatenate(parts)
    order = [offset for held in offsets for offset in held]
    where = [order.index(offset) for offset in range(len(order))]
    blocks = jnp.take(blocks, jnp.array(where)[track ^ jnp.arange(len(order))], axis=0)
    count, four, cols, part = blocks.shape
    return blocks.transpose(1, 0, 2, 3).reshape(1, four, count * cols, part)


def cut_blocks(joined, count, track):
    _, four, width, part = joined.shape
    blocks = joined.reshape(four, count, width // count, part).transpose(1, 0, 2, 3)
    slots = [send_slot(offset, count) for offset in range(count)]
    order = [slots.index(slot) for slot in range(count)]
    return jnp.take(blocks, track ^ jnp.array(order), axis=0)


def stack_blocks(parts):
    def kernel(*refs):
        at = 0
        for ref in refs[:-1]:
            refs[-1][at : at + ref.shape[0]] = ref[...]
            at += ref.shape[0]

    vmem = pl.BlockSpec(memory_space=pltpu.VMEM)
    shape = (sum(part.shape[0] for part in parts),) + parts[0].shape[1:]
    return pl.pallas_call(
        kernel,
        out_shape=jax.ShapeDtypeStruct(shape, BF),
        in_specs=[vmem] * len(parts),
        out_specs=vmem,
        compiler_params=pltpu.CompilerParams(vmem_limit_bytes=16 * 2**20),
    )(*parts)


def gather_blocks(block, axis, other):
    count = lax.axis_size(axis)
    held, order, bit = block[None], [0], count // 2
    while bit > 8:
        held = jnp.concatenate([held, swap(held, axis, bit)])
        order = order + [offset ^ bit for offset in order]
        bit //= 2
    far = [bits for bits in (8, 4, 12) if bits < 2 * bit]
    moved = [swap(held, axis, bits) for bits in far]
    held, other = lax.optimization_barrier((stack_blocks([held]), other))
    moved[0], other = lax.optimization_barrier((moved[0], other))
    held = stack_blocks([held] + moved)
    order = order + [offset ^ bits for bits in far for offset in order]
    parts = [swap(held, axis, bits) if bits else held for bits in range(4)]
    return parts, [[offset ^ bits for offset in order] for bits in range(4)], other


def scatter_sum(blocks, axis):
    count = lax.axis_size(axis)
    blocks = blocks.reshape((4, count // 4) + blocks.shape[1:])
    half = blocks.shape[1] // 2

    def plane_sum(blocks):
        moved = [swap(blocks[bits], axis, bits) for bits in (2, 3, 1)]
        return blocks[0].astype(F32) + sum(block.astype(F32) for block in moved)

    far, close = plane_sum(blocks[:, half:]), plane_sum(blocks[:, :half])
    bit = count // 2
    while bit > 8:
        total = close + swap(far.astype(BF), axis, bit).astype(F32)
        half //= 2
        far, close = total[half:], total[:half]
        bit //= 2
    moved = [swap(far[at].astype(BF), axis, 8 + 4 * at) for at in range(2)]
    return [close[0], swap(close[1].astype(BF), axis, 4)] + moved


def shards(fields, upstream, ln_gain, weights):
    groups, count = lax.axis_size("grp"), lax.axis_size("trk")
    rows_dev, trk_dev, width = fields.shape
    _, part, cols = weights.shape
    cell_count = rows_dev * groups * trk_dev * count
    group, track = lax.axis_index("grp"), lax.axis_index("trk")
    both = jnp.concatenate([fields, upstream], 1)
    gain = jnp.broadcast_to(ln_gain, (8, width))
    place = jnp.stack([group, track]).astype(jnp.int32)
    place, gain, both = lax.optimization_barrier((place, gain, both))
    parts, offsets, both = gather_blocks(weights.transpose(0, 2, 1), "trk", both)
    row = lax.all_to_all(both, "trk", split_axis=0, concat_axis=0, tiled=True)
    out_shape = (count, 4, cols, part)
    narrow = cols % 16 != 0
    if narrow:
        parts, offsets = [join_blocks(parts, offsets, track)], [[0]]
        out_shape = (1, 4, count * cols, part)
    w_parts = [
        lax.ppermute(held, "grp", ring(groups, k)) if k else held
        for k in range(groups)
        for held in parts
    ]
    vmem = pl.BlockSpec(memory_space=pltpu.VMEM)
    smem = pl.BlockSpec(memory_space=pltpu.SMEM)
    length = trk_dev * count
    wg_shape = jax.ShapeDtypeStruct(out_shape, BF)
    scratch = [pltpu.VMEM((groups, length, part), BF)] * 2
    *wg, grads, attended, w_all, gain = pl.pallas_call(
        functools.partial(attend_kernel, groups, offsets),
        out_shape=(wg_shape,) * (groups - 1)
        + (
            jax.ShapeDtypeStruct((3, length, width), BF),
            jax.ShapeDtypeStruct((length, width), BF),
            jax.ShapeDtypeStruct((4, width, width), BF),
            jax.ShapeDtypeStruct((1, width), F32),
        ),
        in_specs=[smem] + [vmem] * (2 + len(w_parts)),
        out_specs=(vmem,) * (groups + 3),
        scratch_shapes=scratch,
        compiler_params=pltpu.CompilerParams(vmem_limit_bytes=48 * 2**20),
    )(place, row, gain, *w_parts)
    own, cells = pl.pallas_call(
        functools.partial(cells_kernel, groups),
        out_shape=(
            wg_shape,
            jax.ShapeDtypeStruct((length, width + 2 * width // trk_dev), BF),
        ),
        in_specs=[smem] + [vmem] * 5,
        out_specs=(vmem, vmem),
        scratch_shapes=scratch,
        compiler_params=pltpu.CompilerParams(vmem_limit_bytes=48 * 2**20),
        cost_estimate=pl.CostEstimate(
            flops=10 * length * width * width, bytes_accessed=16 * width * width, transcendentals=0
        ),
    )(place, row, gain, w_all, grads, attended)
    wg = [own] + list(wg)
    if narrow:
        wg = [cut_blocks(blocks, count, track) for blocks in wg]
    back = lax.all_to_all(cells, "trk", split_axis=0, concat_axis=0, tiled=True)
    total = wg[0].astype(F32)
    for k in range(1, groups):
        total = total + lax.ppermute(wg[k], "grp", ring(groups, k)).astype(F32)
    terms = scatter_sum(total.astype(BF), "trk")
    terms[3], back = lax.optimization_barrier((terms[3], back))
    grad_fields = back[:, :width].reshape(count, trk_dev, width)
    gain_sum = jnp.sum(back[:, width:].astype(F32).reshape(count, 2, width), (0, 1))
    if groups == 2:
        gain_sum = gain_sum + lax.ppermute(gain_sum, "grp", ring(2, 1))
    else:
        gain_sum = jnp.sum(lax.all_gather(gain_sum, "grp"), 0)
    factor = float(cell_count) ** (-0.5)
    gain_sum = gain_sum * factor
    terms[1], terms[2], grad_fields, gain_sum = lax.optimization_barrier(
        (terms[1], terms[2], grad_fields, gain_sum)
    )
    total = sum(term.astype(F32) for term in terms)
    return (grad_fields, total.transpose(0, 2, 1) * factor, gain_sum)


def solution(mesh):
    in_specs = (P("grp", "trk", None), P("grp", "trk", None), P(), P(None, "grp", "trk"))
    out_specs = (P("grp", "trk", None), P(None, "grp", "trk"), P())
    return jax.shard_map(shards, mesh=mesh, in_specs=in_specs, out_specs=out_specs, check_vma=False)
```

```python
import functools

import jax
import jax.numpy as jnp
from jax import lax
from jax.experimental import pallas as pl
from jax.experimental.pallas import tpu as pltpu
from jax.sharding import PartitionSpec as P

HEADS = 8
BF = jnp.bfloat16
F32 = jnp.float32


def dot(a, b, dims):
    return lax.dot_general(a, b, (dims, ((), ())), preferred_element_type=F32)


def send_slot(offset, count):
    return (offset & 3) * (count // 4) + offset // 4


def join_weights(groups, offsets, group, track, w_refs, w_all):
    for step in range(groups):
        for at, held in enumerate(offsets):
            w_ref = w_refs[step * len(offsets) + at]
            _, _, size, part = w_ref.shape
            owner = lax.rem(group - step + groups, groups)
            lanes = pl.ds(pl.multiple_of(owner * part, part), part)
            for slot, offset in enumerate(held):
                begin = (track ^ offset) * size if len(offsets) > 1 else 0
                rows = pl.ds(pl.multiple_of(begin, size), size)
                for index in range(4):
                    w_all[index, rows, lanes] = w_ref[slot, index]


def read_row(rows_ref):
    senders, pair, width = rows_ref.shape
    tracks = pair // 2
    both = rows_ref[...].astype(F32)
    return [both[:, at : at + tracks].reshape(senders * tracks, width) for at in (0, tracks)]


def normalize(values, gain):
    row_mean = jnp.mean(values, -1, keepdims=True)
    offset = values - row_mean
    row_var = jnp.mean(offset * offset, -1, keepdims=True)
    inv_std = lax.rsqrt(row_var + 1e-05)
    centred = offset * inv_std
    return (centred * gain).astype(BF), centred, inv_std


def write_grads(track, wg_ref, grads, up, norm_part, att_part):
    count, _, cols, part = wg_ref.shape
    for index in range(4):
        if index < 3:
            block = dot(grads[index], norm_part, ((0,), (0,))).astype(BF)
        else:
            block = dot(up, att_part, ((0,), (0,))).astype(BF)
        block = block.reshape(count, cols, part)
        for to in range(count):
            slot = send_slot(track ^ to, count) if count > 1 else 0
            wg_ref[slot, index] = block[to]


def pick(array, group, groups, scratch):
    part = array.shape[1] // groups
    for at in range(groups):
        scratch[at] = array[:, at * part : (at + 1) * part]
    return scratch[group]


def attend_kernel(groups, offsets, place, rows_ref, gain_ref, *refs):
    held = groups * len(offsets)
    w_refs, wg_refs, refs = refs[:held], refs[held : held + groups - 1], refs[held + groups - 1 :]
    grads_ref, att_ref, w_all, same_gain_ref, norm_s, att_s = refs
    group, track = place[0], place[1]
    join_weights(groups, offsets, group, track, w_refs, w_all)
    values, upstream = read_row(rows_ref)
    length, width = values.shape
    normed, _, _ = normalize(values, gain_ref[...][:1])
    up = upstream.astype(BF)
    projected = [dot(normed, w_all[index], ((1,), (1,))).astype(BF) for index in range(3)]
    grad_att = dot(up, w_all[3], ((1,), (0,))).astype(BF)
    size = width // HEADS
    scaling = size ** (-0.5)
    span = 2 * size
    lane = lax.broadcasted_iota(jnp.int32, (length, span), 1)
    first = lane < size
    spans = [slice(at, at + span) for at in range(0, width, span)]
    query, keyed, valued = [[member[:, at] for at in spans] for member in projected]
    grad_out = [grad_att[:, at] for at in spans]
    zero = jnp.zeros((length, span), BF)

    def apart(member):
        return jnp.concatenate([jnp.where(first, member, zero), jnp.where(first, zero, member)], 0)

    def together(member):
        return jnp.where(first, member[:length], member[length:]).astype(BF)

    query2, grad2 = [apart(m) for m in query], [apart(m) for m in grad_out]
    scores = [dot(k, q, ((1,), (1,))) * scaling for k, q in zip(keyed, query2)]
    dprobs = [dot(v, g, ((1,), (1,))) for v, g in zip(valued, grad2)]
    shifted = [jnp.exp(s - jnp.max(s, 0, keepdims=True)) for s in scores]
    prob = [s * (1.0 / jnp.sum(s, 0, keepdims=True)) for s in shifted]
    prob_low = [p.astype(BF) for p in prob]
    row_dot = [jnp.sum(p * d, 0, keepdims=True) for p, d in zip(prob, dprobs)]
    score_grad = [
        (p * (d - r) * scaling).astype(BF) for p, d, r in zip(prob, dprobs, row_dot)
    ]
    pieces = [
        [together(dot(s, k, ((0,), (0,)))) for s, k in zip(score_grad, keyed)],
        [dot(s, q, ((1,), (0,))).astype(BF) for s, q in zip(score_grad, query2)],
        [dot(p, g, ((1,), (0,))).astype(BF) for p, g in zip(prob_low, grad2)],
        [together(dot(p, v, ((0,), (0,)))) for p, v in zip(prob_low, valued)],
    ]
    grads = [jnp.concatenate(piece, 1) for piece in pieces[:3]]
    attended = jnp.concatenate(pieces[3], 1)
    for step in range(1, groups):
        owner = lax.rem(group + step, groups)
        write_grads(
            track,
            wg_refs[step - 1],
            grads,
            up,
            pick(normed, owner, groups, norm_s),
            pick(attended, owner, groups, att_s),
        )
    for index in range(3):
        grads_ref[index] = grads[index]
    att_ref[...] = attended
    same_gain_ref[...] = gain_ref[...][:1]


def cells_kernel(groups, place, rows_ref, gain_ref, w_all, grads_ref, att_ref, wg_ref, cells_ref, norm_s, att_s):
    group, track = place[0], place[1]
    values, upstream = read_row(rows_ref)
    senders, tracks = rows_ref.shape[0], rows_ref.shape[1] // 2
    length, width = values.shape
    gain = gain_ref[...]
    normed, centred, inv_std = normalize(values, gain)
    grads = [grads_ref[index] for index in range(3)]
    grad_normed = sum(dot(grads[index], w_all[index], ((1,), (0,))) for index in range(3))
    gain_term = jnp.sum(grad_normed * centred, 0, keepdims=True)
    scaled = grad_normed * gain
    branch = inv_std * (
        scaled
        - jnp.mean(scaled, -1, keepdims=True)
        - centred * jnp.mean(scaled * centred, -1, keepdims=True)
    )
    cells = upstream + branch.astype(BF).astype(F32)
    high = gain_term.astype(BF).astype(F32)
    terms = jnp.concatenate([high, gain_term - high], 1)
    lanes = 2 * width // tracks
    terms = jnp.concatenate([terms[:, at * lanes : (at + 1) * lanes] for at in range(tracks)], 0)
    terms = jnp.broadcast_to(terms[None], (senders, tracks, lanes)).reshape(length, lanes)
    cells_ref[...] = jnp.concatenate([cells, terms], 1).astype(BF)
    write_grads(
        track,
        wg_ref,
        grads,
        upstream.astype(BF),
        pick(normed, group, groups, norm_s),
        pick(att_ref[...], group, groups, att_s),
    )


def finish_kernel(count, factor, *refs):
    terms, gains, (total_ref, gain_ref) = refs[:count], refs[count:-2], refs[-2:]
    total_ref[...] = sum(term[...].astype(F32) for term in terms) * factor
    gain_ref[...] = sum(gain[...] for gain in gains) * factor


def ring(size, step):
    return [(i, (i + step) % size) for i in range(size)]


def swap(array, axis, bits):
    return lax.ppermute(array, axis, [(i, i ^ bits) for i in range(lax.axis_size(axis))])


def join_blocks(parts, offsets, track):
    blocks = jnp.concatenate(parts)
    order = [offset for held in offsets for offset in held]
    where = [order.index(offset) for offset in range(len(order))]
    blocks = jnp.take(blocks, jnp.array(where)[track ^ jnp.arange(len(order))], axis=0)
    count, four, cols, part = blocks.shape
    return blocks.transpose(1, 0, 2, 3).reshape(1, four, count * cols, part)


def cut_blocks(joined, count, track):
    _, four, width, part = joined.shape
    blocks = joined.reshape(four, count, width // count, part).transpose(1, 0, 2, 3)
    slots = [send_slot(offset, count) for offset in range(count)]
    order = [slots.index(slot) for slot in range(count)]
    return jnp.take(blocks, track ^ jnp.array(order), axis=0)


def stack_blocks(parts):
    def kernel(*refs):
        at = 0
        for ref in refs[:-1]:
            refs[-1][at : at + ref.shape[0]] = ref[...]
            at += ref.shape[0]

    vmem = pl.BlockSpec(memory_space=pltpu.VMEM)
    shape = (sum(part.shape[0] for part in parts),) + parts[0].shape[1:]
    return pl.pallas_call(
        kernel,
        out_shape=jax.ShapeDtypeStruct(shape, BF),
        in_specs=[vmem] * len(parts),
        out_specs=vmem,
        compiler_params=pltpu.CompilerParams(vmem_limit_bytes=16 * 2**20),
    )(*parts)


def gather_blocks(block, axis, other):
    count = lax.axis_size(axis)
    held, order, bit = block[None], [0], count // 2
    while bit > 8:
        held = jnp.concatenate([held, swap(held, axis, bit)])
        order = order + [offset ^ bit for offset in order]
        bit //= 2
    far = [bits for bits in (8, 4, 12) if bits < 2 * bit]
    moved = [swap(held, axis, bits) for bits in far]
    held, other = lax.optimization_barrier((stack_blocks([held]), other))
    moved[0], other = lax.optimization_barrier((moved[0], other))
    held = stack_blocks([held] + moved)
    order = order + [offset ^ bits for bits in far for offset in order]
    parts = [swap(held, axis, bits) if bits else held for bits in range(4)]
    return parts, [[offset ^ bits for offset in order] for bits in range(4)], other


def scatter_sum(blocks, axis):
    count = lax.axis_size(axis)
    blocks = blocks.reshape((4, count // 4) + blocks.shape[1:])
    half = blocks.shape[1] // 2

    def plane_sum(blocks):
        moved = [swap(blocks[bits], axis, bits) for bits in (2, 3, 1)]
        return blocks[0].astype(F32) + sum(block.astype(F32) for block in moved)

    far, close = plane_sum(blocks[:, half:]), plane_sum(blocks[:, :half])
    bit = count // 2
    while bit > 8:
        total = close + swap(far.astype(BF), axis, bit).astype(F32)
        half //= 2
        far, close = total[half:], total[:half]
        bit //= 2
    moved = [swap(far[at].astype(BF), axis, 8 + 4 * at) for at in range(2)]
    return [close[0], swap(close[1].astype(BF), axis, 4)] + moved


def shards(fields, upstream, ln_gain, weights):
    groups, count = lax.axis_size("grp"), lax.axis_size("trk")
    rows_dev, trk_dev, width = fields.shape
    _, part, cols = weights.shape
    cell_count = rows_dev * groups * trk_dev * count
    group, track = lax.axis_index("grp"), lax.axis_index("trk")
    both = jnp.concatenate([fields, upstream], 1)
    gain = jnp.broadcast_to(ln_gain, (8, width))
    place = jnp.stack([group, track]).astype(jnp.int32)
    place, gain, both = lax.optimization_barrier((place, gain, both))
    parts, offsets, both = gather_blocks(weights.transpose(0, 2, 1), "trk", both)
    row = lax.all_to_all(both, "trk", split_axis=0, concat_axis=0, tiled=True)
    out_shape = (count, 4, cols, part)
    narrow = cols % 16 != 0
    if narrow:
        parts, offsets = [join_blocks(parts, offsets, track)], [[0]]
        out_shape = (1, 4, count * cols, part)
    w_parts = [
        lax.ppermute(held, "grp", ring(groups, k)) if k else held
        for k in range(groups)
        for held in parts
    ]
    vmem = pl.BlockSpec(memory_space=pltpu.VMEM)
    smem = pl.BlockSpec(memory_space=pltpu.SMEM)
    length = trk_dev * count
    wg_shape = jax.ShapeDtypeStruct(out_shape, BF)
    scratch = [pltpu.VMEM((groups, length, part), BF)] * 2
    *wg, grads, attended, w_all, gain = pl.pallas_call(
        functools.partial(attend_kernel, groups, offsets),
        out_shape=(wg_shape,) * (groups - 1)
        + (
            jax.ShapeDtypeStruct((3, length, width), BF),
            jax.ShapeDtypeStruct((length, width), BF),
            jax.ShapeDtypeStruct((4, width, width), BF),
            jax.ShapeDtypeStruct((1, width), F32),
        ),
        in_specs=[smem] + [vmem] * (2 + len(w_parts)),
        out_specs=(vmem,) * (groups + 3),
        scratch_shapes=scratch,
        compiler_params=pltpu.CompilerParams(vmem_limit_bytes=48 * 2**20),
    )(place, row, gain, *w_parts)
    own, cells = pl.pallas_call(
        functools.partial(cells_kernel, groups),
        out_shape=(
            wg_shape,
            jax.ShapeDtypeStruct((length, width + 2 * width // trk_dev), BF),
        ),
        in_specs=[smem] + [vmem] * 5,
        out_specs=(vmem, vmem),
        scratch_shapes=scratch,
        compiler_params=pltpu.CompilerParams(vmem_limit_bytes=48 * 2**20),
        cost_estimate=pl.CostEstimate(
            flops=10 * length * width * width, bytes_accessed=16 * width * width, transcendentals=0
        ),
    )(place, row, gain, w_all, grads, attended)
    wg = [own] + list(wg)
    if narrow:
        wg = [cut_blocks(blocks, count, track) for blocks in wg]
    back = lax.all_to_all(cells, "trk", split_axis=0, concat_axis=0, tiled=True)
    total = wg[0].astype(F32)
    for k in range(1, groups):
        total = total + lax.ppermute(wg[k], "grp", ring(groups, k)).astype(F32)
    terms = scatter_sum(total.astype(BF), "trk")
    terms[3], back = lax.optimization_barrier((terms[3], back))
    grad_fields = back[:, :width].reshape(count, trk_dev, width)
    gain_sum = jnp.sum(back[:, width:].astype(F32).reshape(count, 2, width), (0, 1))
    if groups == 2:
        gains = [gain_sum, lax.ppermute(gain_sum, "grp", ring(2, 1))]
    else:
        gains = [jnp.sum(lax.all_gather(gain_sum, "grp"), 0)]
    factor = float(cell_count) ** (-0.5)
    terms[1], terms[2], grad_fields, gains[0] = lax.optimization_barrier(
        (terms[1], terms[2], grad_fields, gains[0])
    )
    total, gain_sum = pl.pallas_call(
        functools.partial(finish_kernel, len(terms), factor),
        out_shape=(
            jax.ShapeDtypeStruct(terms[0].shape, F32),
            jax.ShapeDtypeStruct((1, width), F32),
        ),
        in_specs=[vmem] * (len(terms) + len(gains)),
        out_specs=(vmem, vmem),
        compiler_params=pltpu.CompilerParams(vmem_limit_bytes=16 * 2**20),
    )(*[term.astype(F32) if narrow else term for term in terms], *[gain[None] for gain in gains])
    return (grad_fields, total.transpose(0, 2, 1), gain_sum[0])


def solution(mesh):
    in_specs = (P("grp", "trk", None), P("grp", "trk", None), P(), P(None, "grp", "trk"))
    out_specs = (P("grp", "trk", None), P(None, "grp", "trk"), P())
    return jax.shard_map(shards, mesh=mesh, in_specs=in_specs, out_specs=out_specs, check_vma=False)
```

```python
import functools

import jax
import jax.numpy as jnp
from jax import lax
from jax.experimental import pallas as pl
from jax.experimental.pallas import tpu as pltpu
from jax.sharding import PartitionSpec as P

HEADS = 8
BF = jnp.bfloat16
F32 = jnp.float32


def dot(a, b, dims):
    return lax.dot_general(a, b, (dims, ((), ())), preferred_element_type=F32)


def send_slot(offset, count):
    return (offset & 3) * (count // 4) + offset // 4


def join_weights(groups, offsets, group, track, w_refs, w_all):
    for step in range(groups):
        for at, held in enumerate(offsets):
            w_ref = w_refs[step * len(offsets) + at]
            _, _, size, part = w_ref.shape
            owner = lax.rem(group - step + groups, groups)
            lanes = pl.ds(pl.multiple_of(owner * part, part), part)
            for slot, offset in enumerate(held):
                begin = (track ^ offset) * size if len(offsets) > 1 else 0
                rows = pl.ds(pl.multiple_of(begin, size), size)
                for index in range(4):
                    w_all[index, rows, lanes] = w_ref[slot, index]


def read_row(rows_ref):
    senders, pair, width = rows_ref.shape
    tracks = pair // 2
    both = rows_ref[...].astype(F32)
    return [both[:, at : at + tracks].reshape(senders * tracks, width) for at in (0, tracks)]


def normalize(values, gain):
    row_mean = jnp.mean(values, -1, keepdims=True)
    offset = values - row_mean
    row_var = jnp.mean(offset * offset, -1, keepdims=True)
    inv_std = lax.rsqrt(row_var + 1e-05)
    centred = offset * inv_std
    return (centred * gain).astype(BF), centred, inv_std


def write_grads(track, wg_ref, grads, up, norm_part, att_part):
    count, _, cols, part = wg_ref.shape
    for index in range(4):
        if index < 3:
            block = dot(grads[index], norm_part, ((0,), (0,))).astype(BF)
        else:
            block = dot(up, att_part, ((0,), (0,))).astype(BF)
        block = block.reshape(count, cols, part)
        for to in range(count):
            slot = send_slot(track ^ to, count) if count > 1 else 0
            wg_ref[slot, index] = block[to]


def pick(array, group, groups, scratch):
    part = array.shape[1] // groups
    for at in range(groups):
        scratch[at] = array[:, at * part : (at + 1) * part]
    return scratch[group]


def attend_kernel(groups, offsets, place, rows_ref, gain_ref, *refs):
    held = groups * len(offsets)
    w_refs, wg_refs, refs = refs[:held], refs[held : held + groups - 1], refs[held + groups - 1 :]
    grads_ref, att_ref, w_all, same_gain_ref, norm_s, att_s = refs
    group, track = place[0], place[1]
    join_weights(groups, offsets, group, track, w_refs, w_all)
    values, upstream = read_row(rows_ref)
    length, width = values.shape
    normed, _, _ = normalize(values, gain_ref[...][:1])
    up = upstream.astype(BF)
    projected = [dot(normed, w_all[index], ((1,), (1,))).astype(BF) for index in range(3)]
    grad_att = dot(up, w_all[3], ((1,), (0,))).astype(BF)
    size = width // HEADS
    scaling = size ** (-0.5)
    span = 2 * size
    lane = lax.broadcasted_iota(jnp.int32, (length, span), 1)
    first = lane < size
    spans = [slice(at, at + span) for at in range(0, width, span)]
    query, keyed, valued = [[member[:, at] for at in spans] for member in projected]
    grad_out = [grad_att[:, at] for at in spans]
    zero = jnp.zeros((length, span), BF)

    def apart(member):
        return jnp.concatenate([jnp.where(first, member, zero), jnp.where(first, zero, member)], 0)

    def together(member):
        return jnp.where(first, member[:length], member[length:]).astype(BF)

    query2, grad2 = [apart(m) for m in query], [apart(m) for m in grad_out]
    scores = [dot(k, q, ((1,), (1,))) * scaling for k, q in zip(keyed, query2)]
    dprobs = [dot(v, g, ((1,), (1,))) for v, g in zip(valued, grad2)]
    shifted = [jnp.exp(s - jnp.max(s, 0, keepdims=True)) for s in scores]
    prob = [s * (1.0 / jnp.sum(s, 0, keepdims=True)) for s in shifted]
    prob_low = [p.astype(BF) for p in prob]
    row_dot = [jnp.sum(p * d, 0, keepdims=True) for p, d in zip(prob, dprobs)]
    score_grad = [
        (p * (d - r) * scaling).astype(BF) for p, d, r in zip(prob, dprobs, row_dot)
    ]
    pieces = [
        [together(dot(s, k, ((0,), (0,)))) for s, k in zip(score_grad, keyed)],
        [dot(s, q, ((1,), (0,))).astype(BF) for s, q in zip(score_grad, query2)],
        [dot(p, g, ((1,), (0,))).astype(BF) for p, g in zip(prob_low, grad2)],
        [together(dot(p, v, ((0,), (0,)))) for p, v in zip(prob_low, valued)],
    ]
    grads = [jnp.concatenate(piece, 1) for piece in pieces[:3]]
    attended = jnp.concatenate(pieces[3], 1)
    for step in range(1, groups):
        owner = lax.rem(group + step, groups)
        write_grads(
            track,
            wg_refs[step - 1],
            grads,
            up,
            pick(normed, owner, groups, norm_s),
            pick(attended, owner, groups, att_s),
        )
    for index in range(3):
        grads_ref[index] = grads[index]
    att_ref[...] = attended
    same_gain_ref[...] = gain_ref[...][:1]


def cells_kernel(groups, place, rows_ref, gain_ref, w_all, grads_ref, att_ref, wg_ref, cells_ref, norm_s, att_s):
    group, track = place[0], place[1]
    values, upstream = read_row(rows_ref)
    senders, tracks = rows_ref.shape[0], rows_ref.shape[1] // 2
    length, width = values.shape
    gain = gain_ref[...]
    normed, centred, inv_std = normalize(values, gain)
    grads = [grads_ref[index] for index in range(3)]
    grad_normed = sum(dot(grads[index], w_all[index], ((1,), (0,))) for index in range(3))
    gain_term = jnp.sum(grad_normed * centred, 0, keepdims=True)
    scaled = grad_normed * gain
    branch = inv_std * (
        scaled
        - jnp.mean(scaled, -1, keepdims=True)
        - centred * jnp.mean(scaled * centred, -1, keepdims=True)
    )
    cells = upstream + branch.astype(BF).astype(F32)
    high = gain_term.astype(BF).astype(F32)
    terms = jnp.concatenate([high, gain_term - high], 1)
    lanes = 2 * width // tracks
    terms = jnp.concatenate([terms[:, at * lanes : (at + 1) * lanes] for at in range(tracks)], 0)
    terms = jnp.broadcast_to(terms[None], (senders, tracks, lanes)).reshape(length, lanes)
    cells_ref[...] = jnp.concatenate([cells, terms], 1).astype(BF)
    write_grads(
        track,
        wg_ref,
        grads,
        upstream.astype(BF),
        pick(normed, group, groups, norm_s),
        pick(att_ref[...], group, groups, att_s),
    )


def finish_kernel(count, factor, *refs):
    terms, gains, (total_ref, gain_ref) = refs[:count], refs[count:-2], refs[-2:]
    total_ref[...] = sum(term[...].astype(F32) for term in terms) * factor
    gain_ref[...] = sum(gain[...] for gain in gains) * factor


def ring(size, step):
    return [(i, (i + step) % size) for i in range(size)]


def swap(array, axis, bits):
    return lax.ppermute(array, axis, [(i, i ^ bits) for i in range(lax.axis_size(axis))])


def join_blocks(parts, offsets, track):
    blocks = jnp.concatenate(parts)
    order = [offset for held in offsets for offset in held]
    where = [order.index(offset) for offset in range(len(order))]
    blocks = jnp.take(blocks, jnp.array(where)[track ^ jnp.arange(len(order))], axis=0)
    count, four, cols, part = blocks.shape
    return blocks.transpose(1, 0, 2, 3).reshape(1, four, count * cols, part)


def cut_blocks(joined, count, track):
    _, four, width, part = joined.shape
    blocks = joined.reshape(four, count, width // count, part).transpose(1, 0, 2, 3)
    slots = [send_slot(offset, count) for offset in range(count)]
    order = [slots.index(slot) for slot in range(count)]
    return jnp.take(blocks, track ^ jnp.array(order), axis=0)


def stack_blocks(parts):
    def kernel(*refs):
        at = 0
        for ref in refs[:-1]:
            refs[-1][at : at + ref.shape[0]] = ref[...]
            at += ref.shape[0]

    vmem = pl.BlockSpec(memory_space=pltpu.VMEM)
    shape = (sum(part.shape[0] for part in parts),) + parts[0].shape[1:]
    return pl.pallas_call(
        kernel,
        out_shape=jax.ShapeDtypeStruct(shape, BF),
        in_specs=[vmem] * len(parts),
        out_specs=vmem,
        compiler_params=pltpu.CompilerParams(vmem_limit_bytes=16 * 2**20),
    )(*parts)


def gather_blocks(block, axis, other):
    count = lax.axis_size(axis)
    held, order, bit = block[None], [0], count // 2
    while bit > 8:
        held = jnp.concatenate([held, swap(held, axis, bit)])
        order = order + [offset ^ bit for offset in order]
        bit //= 2
    far = [bits for bits in (8, 4, 12) if bits < 2 * bit]
    moved = [swap(held, axis, bits) for bits in far]
    held, other = lax.optimization_barrier((stack_blocks([held]), other))
    moved[0], other = lax.optimization_barrier((moved[0], other))
    held = stack_blocks([held] + moved)
    order = order + [offset ^ bits for bits in far for offset in order]
    first, second = swap(held, axis, 1), swap(held, axis, 2)
    half = len(order) // 2
    parts = [held, first, second, swap(first[:half], axis, 2), swap(second[half:], axis, 1)]
    where = [order, [o ^ 1 for o in order], [o ^ 2 for o in order]]
    where += [[o ^ 3 for o in order[:half]], [o ^ 3 for o in order[half:]]]
    return parts, where, other


def scatter_sum(blocks, axis):
    count = lax.axis_size(axis)
    blocks = blocks.reshape((4, count // 4) + blocks.shape[1:])
    half = blocks.shape[1] // 2

    def plane_sum(blocks, order):
        moved = [swap(blocks[bits], axis, bits) for bits in order]
        return blocks[0].astype(F32) + sum(block.astype(F32) for block in moved)

    far, close = plane_sum(blocks[:, half:], (1, 3, 2)), plane_sum(blocks[:, :half], (3, 1, 2))
    bit = count // 2
    while bit > 8:
        total = close + swap(far.astype(BF), axis, bit).astype(F32)
        half //= 2
        far, close = total[half:], total[:half]
        bit //= 2
    moved = [swap(far[at].astype(BF), axis, 8 + 4 * at) for at in range(2)]
    return [close[0], swap(close[1].astype(BF), axis, 4)] + moved


def shards(fields, upstream, ln_gain, weights):
    groups, count = lax.axis_size("grp"), lax.axis_size("trk")
    rows_dev, trk_dev, width = fields.shape
    _, part, cols = weights.shape
    cell_count = rows_dev * groups * trk_dev * count
    group, track = lax.axis_index("grp"), lax.axis_index("trk")
    both = jnp.concatenate([fields, upstream], 1)
    gain = jnp.broadcast_to(ln_gain, (8, width))
    place = jnp.stack([group, track]).astype(jnp.int32)
    place, gain, both = lax.optimization_barrier((place, gain, both))
    parts, offsets, both = gather_blocks(weights.transpose(0, 2, 1), "trk", both)
    row = lax.all_to_all(both, "trk", split_axis=0, concat_axis=0, tiled=True)
    out_shape = (count, 4, cols, part)
    narrow = cols % 16 != 0
    if narrow:
        parts, offsets = [join_blocks(parts, offsets, track)], [[0]]
        out_shape = (1, 4, count * cols, part)
    w_parts = [
        lax.ppermute(held, "grp", ring(groups, k)) if k else held
        for k in range(groups)
        for held in parts
    ]
    vmem = pl.BlockSpec(memory_space=pltpu.VMEM)
    smem = pl.BlockSpec(memory_space=pltpu.SMEM)
    length = trk_dev * count
    wg_shape = jax.ShapeDtypeStruct(out_shape, BF)
    scratch = [pltpu.VMEM((groups, length, part), BF)] * 2
    *wg, grads, attended, w_all, gain = pl.pallas_call(
        functools.partial(attend_kernel, groups, offsets),
        out_shape=(wg_shape,) * (groups - 1)
        + (
            jax.ShapeDtypeStruct((3, length, width), BF),
            jax.ShapeDtypeStruct((length, width), BF),
            jax.ShapeDtypeStruct((4, width, width), BF),
            jax.ShapeDtypeStruct((1, width), F32),
        ),
        in_specs=[smem] + [vmem] * (2 + len(w_parts)),
        out_specs=(vmem,) * (groups + 3),
        scratch_shapes=scratch,
        compiler_params=pltpu.CompilerParams(vmem_limit_bytes=48 * 2**20),
    )(place, row, gain, *w_parts)
    own, cells = pl.pallas_call(
        functools.partial(cells_kernel, groups),
        out_shape=(
            wg_shape,
            jax.ShapeDtypeStruct((length, width + 2 * width // trk_dev), BF),
        ),
        in_specs=[smem] + [vmem] * 5,
        out_specs=(vmem, vmem),
        scratch_shapes=scratch,
        compiler_params=pltpu.CompilerParams(vmem_limit_bytes=48 * 2**20),
        cost_estimate=pl.CostEstimate(
            flops=10 * length * width * width, bytes_accessed=16 * width * width, transcendentals=0
        ),
    )(place, row, gain, w_all, grads, attended)
    wg = [own] + list(wg)
    if narrow:
        wg = [cut_blocks(blocks, count, track) for blocks in wg]
    back = lax.all_to_all(cells, "trk", split_axis=0, concat_axis=0, tiled=True)
    total = wg[0].astype(F32)
    for k in range(1, groups):
        total = total + lax.ppermute(wg[k], "grp", ring(groups, k)).astype(F32)
    terms = scatter_sum(total.astype(BF), "trk")
    terms[3], back = lax.optimization_barrier((terms[3], back))
    grad_fields = back[:, :width].reshape(count, trk_dev, width)
    gain_sum = jnp.sum(back[:, width:].astype(F32).reshape(count, 2, width), (0, 1))
    if groups == 2:
        gains = [gain_sum, lax.ppermute(gain_sum, "grp", ring(2, 1))]
    else:
        gains = [jnp.sum(lax.all_gather(gain_sum, "grp"), 0)]
    factor = float(cell_count) ** (-0.5)
    terms[1], terms[2], grad_fields, gains[0] = lax.optimization_barrier(
        (terms[1], terms[2], grad_fields, gains[0])
    )
    total, gain_sum = pl.pallas_call(
        functools.partial(finish_kernel, len(terms), factor),
        out_shape=(
            jax.ShapeDtypeStruct(terms[0].shape, F32),
            jax.ShapeDtypeStruct((1, width), F32),
        ),
        in_specs=[vmem] * (len(terms) + len(gains)),
        out_specs=(vmem, vmem),
        compiler_params=pltpu.CompilerParams(vmem_limit_bytes=16 * 2**20),
    )(*[term.astype(F32) if narrow else term for term in terms], *[gain[None] for gain in gains])
    return (grad_fields, total.transpose(0, 2, 1), gain_sum[0])


def solution(mesh):
    in_specs = (P("grp", "trk", None), P("grp", "trk", None), P(), P(None, "grp", "trk"))
    out_specs = (P("grp", "trk", None), P(None, "grp", "trk"), P())
    return jax.shard_map(shards, mesh=mesh, in_specs=in_specs, out_specs=out_specs, check_vma=False)
```
